1024 devices in a mesh: dp: 32 (over z_lo, x), mp: 32 (over z_hi, y, core).
Axes of the slice: x: 4, y: 4, z: 32 (z_hi: 4, z_lo: 8; z = z_hi * 8 + z_lo), core: 2. Of those that a mesh axis runs over, the one named last changes fastest.
Arguments:
- patches: bfloat16 [4096, 6144], P('dp', 'mp'), may hold values from -6 to 6
- route_owner: int32 [4096], P('dp'), may hold values from 0 to 31, as said below
- route_slot: int32 [4096], P('dp'), may hold values from 0 to 127, as said below
- segment_ids: int32 [32, 128], P('dp'), may hold values from 0 to 3, never falling along the last dimension, each value on 1 to 64 neighbouring positions
- ln_gain: float32 [6144], replicated, may hold values from 0.25 to 1.75
- qkv_weight: bfloat16 [6144, 12288], P(None, 'mp'), may hold values from -0.078125 to 0.078125
- q_gain: float32 [4096], P('mp'), may hold values from 0.25 to 1.75
- k_gain: float32 [4096], P('mp'), may hold values from 0.25 to 1.75
- d_attn: bfloat16 [4096, 4096], P('dp', 'mp'), may hold values from -6 to 6
Outputs:
- attn_out: bfloat16 [4096, 4096], P('dp', 'mp')
- norm_grad: float32 [6144, 4096], P('mp', 'dp')
- weight_grad: float32 [6144, 12288], P('dp', 'mp')
The draws below stay inside these ranges and needn't reach their ends.
Inputs may be any that keep to these rules, and one draw needn't show every extreme that they name: `route_owner`: of the rows of one device of dp, at most 12 have one owner, and on every draw some device sends exactly 12 rows to some owner and some owner receives exactly 12 from some device; every owner receives exactly 128 rows in all. `route_slot`: together with route_owner, every position of every owner's sequence is named by exactly one row.
All inputs are finite; a program needn't handle non-finite values.
Results may differ from the reference program's by a relative error of at most 0.03.
Values may be sent and summed in bfloat16 or wider, within the bound.
A program may use at most 32 MiB of HBM per device.

```python
import math
import jax
import jax.numpy as jnp
import numpy as np
from jax import lax

D = 6144
HEAD = 128
HEAD_DEV = 1
HEADS = 32
PAIR = 4
ROWS = 128
ROWS_ALL = 4096
IMAGES = 4
N_DP = 32
N_MP = 32


def build_routes(key):
    key = jax.random.fold_in(key, 11)
    subkeys = jax.random.split(key, 5)
    groups = N_DP // 4
    first = jax.random.randint(subkeys[0], (groups,), 0, PAIR + 1)
    second = jax.random.randint(subkeys[1], (groups,), 0, PAIR - first + 1)
    third = PAIR - first - second
    heavy = jnp.full((groups,), 3 * PAIR, jnp.int32)
    pattern = jnp.stack([heavy, first.astype(jnp.int32), second.astype(jnp.int32), third.astype(jnp.int32)], axis=1).reshape(N_DP)
    pattern = pattern[jax.random.permutation(subkeys[2], N_DP)]
    heavy_at = jnp.argmax((pattern == 3 * PAIR).astype(jnp.int32)).astype(jnp.int32)
    moved = pattern[1]
    pattern = pattern.at[heavy_at].set(moved).at[1].set(3 * PAIR)
    source = jnp.arange(N_DP)
    counts = pattern[(source[None, :] - source[:, None]) % N_DP]
    ends = jnp.cumsum(counts, axis=1)
    starts = ends - counts
    places = jnp.arange(ROWS)
    owner_sorted = jnp.sum((ends[:, None, :] <= places[None, :, None]).astype(jnp.int32), axis=2)
    rank_sorted = places[None, :] - jnp.take_along_axis(starts, owner_sorted, axis=1)
    offsets = jnp.cumsum(counts, axis=0) - counts
    arrival = jnp.take_along_axis(offsets, owner_sorted, axis=1) + rank_sorted
    slot_perm = jax.vmap(lambda part_key: jax.random.permutation(part_key, ROWS))(jax.random.split(subkeys[3], N_DP))
    slot_sorted = slot_perm[owner_sorted, arrival]
    row_perm = jax.vmap(lambda part_key: jax.random.permutation(part_key, ROWS))(jax.random.split(subkeys[4], N_DP))
    owner = jnp.take_along_axis(owner_sorted, row_perm, axis=1).reshape(-1)
    slot = jnp.take_along_axis(slot_sorted, row_perm, axis=1).reshape(-1)
    return (owner.astype(jnp.int32), slot.astype(jnp.int32))


def draw_route_owner(key, part):
    shared = build_routes(key)
    return shared[0]


def draw_route_slot(key, part):
    shared = build_routes(key)
    return shared[1]


def levels(rng, shape, cuts, least, top_value):
    def one(dim, parts):
        steps = jax.random.uniform(jax.random.fold_in(jax.random.fold_in(rng, 6), dim), (parts,), jnp.float32, least / len(cuts), top_value / len(cuts))
        return jnp.repeat(jnp.exp(steps), shape[dim] // parts).reshape((-1,) + (1,) * (len(shape) - dim - 1))

    level = one(*cuts[0])
    for cut in cuts[1:]:
        level = level * one(*cut)
    return level


def split_up(number_of, total, bound, lean):
    loads = [(1 << 20) // math.isqrt(rank ** lean) + 1 for rank in range(2, number_of + 1)]
    spare, holding = total - bound - (number_of - 1), [1] * (number_of - 1)
    while spare > 0:
        candidates = [i for i in range(number_of - 1) if holding[i] < bound]
        pool, remaining = sum([loads[i] for i in candidates]), spare
        for i in candidates:
            extra = min(bound - holding[i], max(1, remaining * loads[i] // pool), spare)
            holding[i] = holding[i] + extra
            spare = spare - extra
    return np.array([bound] + holding)


def ragged_sizes(own_key, amount, total, bound, slope):
    if amount == 2:
        one = jax.random.randint(own_key, (), max(1, total - bound), min(bound, total - 1) + 1)
        return jnp.stack([one, total - one])
    tallies = jnp.asarray(split_up(amount, total, bound, slope), jnp.int32)
    twos = (amount - 1) // 2
    donor, sink = tallies[1:1 + 2 * twos:2], tallies[2:2 + 2 * twos:2]
    slack = jnp.minimum(donor - 1, bound - sink)
    moved = jax.random.randint(jax.random.fold_in(own_key, 1), (twos,), 0, 1 << 20) % (slack + 1)
    tallies = tallies.at[1:1 + 2 * twos:2].set(donor - moved).at[2:2 + 2 * twos:2].set(sink + moved)
    return tallies[jax.random.permutation(jax.random.fold_in(own_key, 2), amount)]


def noise(key, shape, deviation, bound, cuts=(), held_as=jnp.bfloat16):
    drawn = deviation * jax.random.normal(key, shape, jnp.float32)
    if cuts:
        drawn = drawn * levels(key, shape, cuts, -0.22, 0.18)
    return jnp.clip(drawn, -bound, bound).astype(held_as)


def setup_inputs(seed: int = 0) -> dict:
    key_list = jax.random.split(jax.random.key(seed), 10)
    return {
        "patches": noise(key_list[0], (ROWS_ALL, D), 1.0, 6.0, ((0, 32), (1, 32))),
        "route_owner": draw_route_owner(jax.random.fold_in(key_list[9], 71), 0),
        "route_slot": draw_route_slot(jax.random.fold_in(key_list[9], 71), 0),
        "segment_ids": jax.vmap(lambda own: jnp.searchsorted(jnp.cumsum(ragged_sizes(own, IMAGES, ROWS, ROWS // 2, 2)), jnp.arange(ROWS), side="right"))(jax.random.split(key_list[3], N_DP)).reshape((N_DP, ROWS)).astype(jnp.int32),
        "ln_gain": jnp.clip(1.0 + 0.15 * jax.random.normal(key_list[4], (D,), jnp.float32), 0.25, 1.75),
        "qkv_weight": noise(key_list[5], (D, 3 * HEADS * HEAD), D ** -0.5, 0.078125, ((1, 32),)),
        "q_gain": jnp.clip(1.0 + 0.15 * jax.random.normal(key_list[6], (HEADS * HEAD,), jnp.float32), 0.25, 1.75),
        "k_gain": jnp.clip(1.0 + 0.15 * jax.random.normal(key_list[7], (HEADS * HEAD,), jnp.float32), 0.25, 1.75),
        "d_attn": noise(key_list[8], (ROWS_ALL, HEADS * HEAD), 1.0, 6.0, ((0, 32), (1, 32))),
    }


def norm_head(vector, gain_row):
    center = vector - lax.optimization_barrier(jnp.mean(vector, axis=-1, keepdims=True))
    inverse = lax.rsqrt(lax.optimization_barrier(jnp.mean(center * center, axis=-1, keepdims=True)) + 1e-06)
    unit_rows = center * inverse
    return (unit_rows * gain_row, unit_rows, inverse)

def norm_head_back(cotangent, unit_rows, inverse, gain_row):
    scaled = cotangent * gain_row
    return inverse * (scaled - lax.optimization_barrier(jnp.mean(scaled, axis=-1, keepdims=True)) - unit_rows * lax.optimization_barrier(jnp.mean(scaled * unit_rows, axis=-1, keepdims=True)))

def head_pass(block, gain_query, gain_key, segments, cotangent):
    size_head = block.shape[1] // 3
    query_raw = block[:, :size_head].astype(jnp.float32)
    key_raw = block[:, size_head:2 * size_head].astype(jnp.float32)
    value_rows = block[:, 2 * size_head:]
    query_n, query_u, query_r = norm_head(query_raw, gain_query)
    key_n, key_u, key_r = norm_head(key_raw, gain_key)
    factor = 1.0 / math.sqrt(size_head)
    scores = jnp.dot(query_n, key_n.T, precision=lax.Precision.HIGHEST) * factor
    allowed = segments[:, None] == segments[None, :]
    scores = jnp.where(allowed, scores, -1e+30)
    shifted = jnp.exp(scores - lax.optimization_barrier(jnp.max(scores, axis=1, keepdims=True)))
    softmax_rows = shifted / lax.optimization_barrier(jnp.sum(shifted, axis=1, keepdims=True))
    probs_low = softmax_rows.astype(jnp.bfloat16)
    attended = jnp.dot(probs_low, value_rows, preferred_element_type=jnp.float32).astype(jnp.bfloat16)
    grad_value = jnp.dot(probs_low.T, cotangent, preferred_element_type=jnp.float32)
    grad_probs = jnp.dot(cotangent, value_rows.T, preferred_element_type=jnp.float32)
    grad_scores = softmax_rows * (grad_probs - lax.optimization_barrier(jnp.sum(grad_probs * softmax_rows, axis=1, keepdims=True)))
    grad_qn = jnp.dot(grad_scores, key_n, precision=lax.Precision.HIGHEST) * factor
    grad_kn = jnp.dot(grad_scores.T, query_n, precision=lax.Precision.HIGHEST) * factor
    grad_query = norm_head_back(grad_qn, query_u, query_r, gain_query)
    grad_key = norm_head_back(grad_kn, key_u, key_r, gain_key)
    joined = jnp.concatenate([grad_query, grad_key, grad_value], axis=1)
    return (attended, joined.astype(jnp.bfloat16))

def reference(patches, route_owner, route_slot, segment_ids, ln_gain, qkv_weight, q_gain, k_gain, d_attn):
    position = (route_owner * ROWS + route_slot).astype(jnp.int32)
    packed = jnp.zeros(patches.shape, patches.dtype).at[position].set(patches)
    values = packed.astype(jnp.float32)
    row_mean = lax.optimization_barrier(jnp.sum(values, axis=1)) / D
    row_var = lax.optimization_barrier(jnp.sum(values * values, axis=1)) / D - row_mean * row_mean
    inverse = lax.rsqrt(row_var + 1e-06)
    normed = ((values - row_mean[:, None]) * inverse[:, None] * ln_gain[None, :]).astype(jnp.bfloat16)
    weight_wide = qkv_weight.astype(jnp.float32).reshape(D, N_MP, HEAD_DEV * 3 * HEAD)
    gains_query = q_gain.reshape(HEADS, HEAD)
    gains_key = k_gain.reshape(HEADS, HEAD)

    def group_step(running, pieces):
        group_rows, group_segments, group_cot = pieces
        projected = jnp.dot(group_rows, qkv_weight, preferred_element_type=jnp.float32).astype(jnp.bfloat16)
        blocks = projected.reshape(ROWS, HEADS, 3 * HEAD).transpose(1, 0, 2)
        cot_heads = group_cot.reshape(ROWS, HEADS, HEAD).transpose(1, 0, 2)
        attended, grads = jax.vmap(head_pass, in_axes=(0, 0, 0, None, 0))(blocks, gains_query, gains_key, group_segments, cot_heads)
        attended = attended.transpose(1, 0, 2).reshape(ROWS, HEADS * HEAD)
        grads = grads.transpose(1, 0, 2).reshape(ROWS, HEADS * 3 * HEAD)
        partial_w = lax.dot_general(group_rows, grads, (((0,), (0,)), ((), ())), preferred_element_type=jnp.float32)
        partial_w = lax.optimization_barrier(partial_w.astype(jnp.bfloat16)).astype(jnp.float32)
        grads_wide = grads.astype(jnp.float32).reshape(ROWS, N_MP, HEAD_DEV * 3 * HEAD)
        terms = jnp.einsum('dmc,rmc->mdr', weight_wide, grads_wide, precision=lax.Precision.HIGHEST)
        terms = lax.optimization_barrier(terms.astype(jnp.bfloat16)).astype(jnp.float32)
        return (running + partial_w, (attended, lax.optimization_barrier(jnp.sum(terms, axis=0))))
    start_w = jnp.zeros((D, HEADS * 3 * HEAD), jnp.float32)
    inputs = (normed.reshape(N_DP, ROWS, D), segment_ids, d_attn.reshape(N_DP, ROWS, HEADS * HEAD))
    weight_grad, (attended, grads_norm) = lax.scan(group_step, start_w, inputs)
    attn_out = attended.reshape(N_DP * ROWS, HEADS * HEAD)
    norm_grad = grads_norm.transpose(1, 0, 2).reshape(D, N_DP * ROWS)
    return (attn_out, norm_grad, weight_grad)
```

```python
import functools
import math

import jax
import jax.numpy as jnp
from jax import lax
from jax.experimental import pallas as pl
from jax.experimental.pallas import tpu as pltpu
from jax.sharding import PartitionSpec as P

MESH = pl.DeviceIdType.MESH
F32 = jnp.float32
BF16 = jnp.bfloat16
HEAD = 128
ROWS = 128
ZL, X = 8, 4
ZH, Y, C = 4, 4, 2
SLOT = 16
HIGHEST = lax.Precision.HIGHEST


def dot(a, b, ca, cb, precision=None):
    return lax.dot_general(
        a, b, (((ca,), (cb,)), ((), ())), precision=precision, preferred_element_type=F32
    )


def rcopy(src, dst, ssem, rsem, dev):
    return pltpu.make_async_remote_copy(
        src_ref=src, dst_ref=dst, send_sem=ssem, recv_sem=rsem, device_id=dev, device_id_type=MESH
    )


class Ring:
    def __init__(self, n, p, dev):
        self.n, self.p = n, p
        self.right = lax.rem(p + 1, n)
        self.left = lax.rem(p + n - 1, n)
        self.opp = lax.rem(p + 2, n)
        self.dev_right, self.dev_left = dev(self.right), dev(self.left)

    def others(self):
        return {1: [], 2: [self.left], 4: [self.opp, self.left, self.right]}[self.n]

    def neighbours(self):
        return {1: [], 2: [self.dev_right], 4: [self.dev_left, self.dev_right]}[self.n]


class Gather:
    def __init__(self, ring, block, half, ss, rs, base):
        self.ring, self.block, self.half = ring, block, half
        self.ss, self.rs, self.base = ss, rs, base

    def _copy(self, ref, i, dev):
        return rcopy(ref, ref, self.ss.at[self.base + i], self.rs.at[self.base + i], dev)

    def _parts(self):
        g = self.ring
        if g.n == 1:
            return []
        if g.n == 2:
            return [(self.block(g.p), g.dev_right)]
        return [
            (self.block(g.p), g.dev_right),
            (self.block(g.p), g.dev_left),
            (self.half(g.left, 0), g.dev_right),
            (self.half(g.right, 1), g.dev_left),
        ]

    def send(self):
        for i, (ref, dev) in enumerate(self._parts()[:2]):
            self._copy(ref, i, dev).start()

    def relay(self):
        g = self.ring
        if g.n == 1:
            return
        self._copy(self.block(g.left), 0, g.dev_right).wait_recv()
        if g.n == 4:
            self._copy(self.half(g.left, 0), 2, g.dev_right).start()
            self._copy(self.block(g.right), 1, g.dev_left).wait_recv()
            self._copy(self.half(g.right, 1), 3, g.dev_left).start()

    def last(self):
        g = self.ring
        if g.n == 4:
            self._copy(self.half(g.opp, 0), 2, g.dev_right).wait_recv()
            self._copy(self.half(g.opp, 1), 3, g.dev_left).wait_recv()

    def drain(self):
        for i, (ref, dev) in enumerate(self._parts()):
            self._copy(ref, i, dev).wait_send()


class Scatter:
    def __init__(self, ring, block, half, bufs, ss, rs, base):
        self.ring, self.block, self.half, self.bufs = ring, block, half, bufs
        self.ss, self.rs, self.base = ss, rs, base

    def _copy(self, ref, i, dev):
        return rcopy(ref, self.bufs[i], self.ss.at[self.base + i], self.rs.at[self.base + i], dev)

    def _parts(self):
        g = self.ring
        if g.n == 1:
            return []
        if g.n == 2:
            return [(2, self.block(g.right), g.dev_right)]
        return [
            (0, self.half(g.opp, 0), g.dev_right),
            (1, self.half(g.opp, 1), g.dev_left),
            (2, self.block(g.right), g.dev_right),
            (3, self.block(g.left), g.dev_left),
        ]

    def first(self):
        for i, ref, dev in self._parts():
            if i < 2:
                self._copy(ref, i, dev).start()

    def second(self):
        g = self.ring
        if g.n == 4:
            self._copy(self.bufs[0], 0, g.dev_right).wait_recv()
            add_to(self.half(g.right, 0), self.bufs[0])
        if g.n > 1:
            self._copy(self.block(g.right), 2, g.dev_right).start()
        if g.n == 4:
            self._copy(self.bufs[1], 1, g.dev_left).wait_recv()
            add_to(self.half(g.left, 1), self.bufs[1])
            self._copy(self.block(g.left), 3, g.dev_left).start()

    def total(self):
        g = self.ring
        out = self.block(g.p)[...].astype(F32)
        if g.n > 1:
            self._copy(self.bufs[2], 2, g.dev_right).wait_recv()
            out = out + self.bufs[2][...].astype(F32)
        if g.n == 4:
            self._copy(self.bufs[3], 3, g.dev_left).wait_recv()
            out = out + self.bufs[3][...].astype(F32)
        return out

    def drain(self):
        for i, ref, dev in self._parts():
            self._copy(ref, i, dev).wait_send()


def add_to(ref, other):
    ref[...] = (ref[...].astype(F32) + other[...].astype(F32)).astype(ref.dtype)


def mean_of(v):
    return jnp.mean(v, axis=1, keepdims=True)


def norm_head(vector, gain_row):
    center = vector - mean_of(vector)
    inverse = lax.rsqrt(mean_of(center * center) + 1e-06)
    unit_rows = center * inverse
    return unit_rows * gain_row, unit_rows, inverse


def norm_head_back(cotangent, unit_rows, inverse, gain_row):
    scaled = cotangent * gain_row
    return inverse * (scaled - mean_of(scaled) - unit_rows * mean_of(scaled * unit_rows))


def head_pass(projected, gain_query, gain_key, allowed, cotangent):
    value_rows = projected[:, 2 * HEAD :]
    query_n, query_u, query_r = norm_head(projected[:, :HEAD].astype(F32), gain_query)
    key_n, key_u, key_r = norm_head(projected[:, HEAD : 2 * HEAD].astype(F32), gain_key)
    factor = 1.0 / math.sqrt(HEAD)
    scores = dot(query_n, key_n, 1, 1, HIGHEST) * factor
    scores = jnp.where(allowed, scores, -1e30)
    shifted = jnp.exp(scores - jnp.max(scores, axis=1, keepdims=True))
    softmax_rows = shifted / jnp.sum(shifted, axis=1, keepdims=True)
    probs_low = softmax_rows.astype(BF16)
    attended = dot(probs_low, value_rows, 1, 0).astype(BF16)
    grad_value = dot(probs_low, cotangent, 0, 0)
    grad_probs = dot(cotangent, value_rows, 1, 1)
    grad_scores = softmax_rows * (
        grad_probs - jnp.sum(grad_probs * softmax_rows, axis=1, keepdims=True)
    )
    grad_qn = dot(grad_scores, key_n, 1, 0, HIGHEST) * factor
    grad_kn = dot(grad_scores, query_n, 0, 0, HIGHEST) * factor
    grad_query = norm_head_back(grad_qn, query_u, query_r, gain_query)
    grad_key = norm_head_back(grad_kn, key_u, key_r, gain_key)
    return attended, jnp.concatenate([grad_query, grad_key, grad_value], axis=1).astype(BF16)


def kernel(
    patches_ref, owner_ref, slot_ref, seg_ref, gain_ref, w_hbm, qg_ref, kg_ref, cot_ref,
    attn_ref, ng_ref, wg_ref,
    w_ref, gb_ref, pt_ref, out_buf, arr, gath, nt, br, ga, ts, cr, ya, yb, yl, yr, qb, za, zb, zl_, zr_,
    w_sem, a2a_s, a2a_r, hg_s, hg_r, yg_s, yg_r, cg_s, cg_r, nt_s, nt_r, ny_s, ny_r, nc_s, nc_r,
    zg_s, zg_r, xg_s, xg_r, ca_s, ca_r, yr_s, yr_r, hr_s, hr_r,
):
    n_dp, n_mp = ZL * X, ZH * Y * C
    feats = patches_ref.shape[0]
    width = n_mp * feats
    fy = feats // Y
    per_class = n_dp // C
    d, m = lax.axis_index("dp"), lax.axis_index("mp")
    z, x = lax.div(d, X), lax.rem(d, X)
    h, y, c = lax.div(m, Y * C), lax.rem(lax.div(m, C), Y), lax.rem(m, C)
    ring_h = Ring(ZH, h, lambda q: (d, (q * Y + y) * C + c))
    ring_y = Ring(Y, y, lambda q: (d, (h * Y + q) * C + c))
    ring_x = Ring(X, x, lambda q: (z * X + q, m))
    twin = (d, (h * Y + y) * C + (1 - c))
    other = 1 - c

    load_w = pltpu.make_async_copy(w_hbm, w_ref, w_sem)
    load_w.start()

    barrier = pltpu.get_barrier_semaphore()

    def hail(k, _):
        to = lax.rem(d + k, n_dp)
        pl.semaphore_signal(barrier, inc=1, device_id=(to, m), device_id_type=MESH)
        return 0

    lax.fori_loop(1, n_dp, hail, 0)
    near = ring_h.neighbours() + ring_y.neighbours() + ([twin] if C == 2 else [])
    for dev in near:
        pl.semaphore_signal(barrier, inc=1, device_id=dev, device_id_type=MESH)

    owners = jnp.broadcast_to(owner_ref[...].astype(F32), (ROWS, ROWS))
    rows_i = lax.broadcasted_iota(jnp.int32, (ROWS, ROWS), 0)
    cols_i = lax.broadcasted_iota(jnp.int32, (ROWS, ROWS), 1)
    same = jnp.where((owners == owners.T) & (rows_i < cols_i), 1.0, 0.0)
    rank = jnp.sum(same, axis=0, keepdims=True)
    target = owner_ref[...].astype(F32) * SLOT + rank
    slots_i = lax.broadcasted_iota(jnp.int32, (n_dp * SLOT, ROWS), 0).astype(F32)
    pick = jnp.where(slots_i == target, 1.0, 0.0).astype(BF16)
    pt_ref[:feats] = patches_ref[...]
    pt_ref[feats:] = jnp.broadcast_to(
        slot_ref[...].astype(F32) + 1.0, (pt_ref.shape[0] - feats, ROWS)
    ).astype(BF16)
    outgoing = dot(pick, pt_ref[...], 1, 1).astype(BF16)
    out_buf[...] = outgoing.reshape(out_buf.shape)

    pl.semaphore_wait(barrier, n_dp - 1 + len(near))

    def a2a_send(k, _):
        to = lax.rem(d + k, n_dp)
        rcopy(out_buf.at[to], arr.at[d], a2a_s.at[to], a2a_r.at[d], (to, m)).start()
        return 0

    lax.fori_loop(1, n_dp, a2a_send, 0)
    arr[d] = out_buf[d]

    def spread_gain(j, _):
        tile = jnp.broadcast_to(gain_ref[pl.ds(j, 1), :], (128, 128))
        gb_ref[pl.ds(pl.multiple_of(j * 128, 128), 128), :] = tile.T
        return 0

    lax.fori_loop(0, width // 128, spread_gain, 0)

    def a2a_wait(k, _):
        frm = lax.rem(d + n_dp - k, n_dp)
        rcopy(out_buf.at[frm], arr.at[frm], a2a_s.at[frm], a2a_r.at[frm], (frm, m)).wait_recv()
        return 0

    lax.fori_loop(1, n_dp, a2a_wait, 0)
    arrived = arr[...].reshape(n_dp * SLOT, arr.shape[2])
    lanes = lax.broadcasted_iota(jnp.int32, (n_dp * SLOT, ROWS), 1).astype(F32) + 1.0
    place = jnp.where(
        lanes == arrived[:, feats : feats + 1].astype(F32), 1.0, 0.0
    ).astype(BF16)
    gath[m] = dot(arrived[:, :feats], place, 0, 0).astype(BF16)

    g_h = Gather(
        ring_h,
        lambda q: gath.at[(q * Y + y) * C + c],
        lambda q, i: gath.at[(q * Y + y) * C + c, pl.ds(i * (feats // 2), feats // 2)],
        hg_s, hg_r, 0,
    )

    def gather_y(idx, hh):
        return Gather(
            ring_y,
            lambda q: gath.at[(hh * Y + q) * C + c],
            lambda q, i: gath.at[(hh * Y + q) * C + c, pl.ds(i * (feats // 2), feats // 2)],
            yg_s, yg_r, idx * 4,
        )

    def twin_copy(idx, hh, q, core):
        ref = gath.at[(hh * Y + q) * C + core]
        i = idx * Y + q
        return rcopy(ref, ref, cg_s.at[i], cg_r.at[i], twin)

    def to_twin(idx, hh, qs):
        if C == 2:
            for q in qs:
                twin_copy(idx, hh, q, c).start()

    come = [h] + {1: [], 2: [ring_h.left], 4: [ring_h.left, ring_h.right, ring_h.opp]}[ZH]
    g_y = [gather_y(i, hh) for i, hh in enumerate(come)]
    near_y = {1: [], 2: [ring_y.left], 4: [ring_y.left, ring_y.right]}[Y]
    far_y = [ring_y.opp] if Y == 4 else []

    def own_y(i):
        g_y[i].send()
        to_twin(i, come[i], [y])

    def next_y(i):
        g_y[i].relay()
        to_twin(i, come[i], near_y)

    def last_y(i):
        g_y[i].last()
        to_twin(i, come[i], far_y)

    g_h.send()
    own_y(0)
    next_y(0)
    g_h.relay()
    for i in range(1, min(len(come), 3)):
        own_y(i)
    last_y(0)
    g_h.last()
    if ZH == 4:
        own_y(3)
    for i in range(1, len(come)):
        next_y(i)
    for i in range(1, len(come)):
        last_y(i)
    if C == 2:
        for i, hh in enumerate(come):
            for q in range(Y):
                twin_copy(i, hh, q, other).wait_recv()

    def sums(j, carry):
        s1, s2 = carry
        v = gath[j].astype(F32).reshape(feats // 8, 8, ROWS)
        return s1 + jnp.sum(v, axis=0), s2 + jnp.sum(v * v, axis=0)

    zero = jnp.zeros((8, ROWS), F32)
    s1, s2 = lax.fori_loop(0, n_mp, sums, (zero, zero))
    row_mean = jnp.sum(s1, axis=0, keepdims=True) / width
    row_var = jnp.sum(s2, axis=0, keepdims=True) / width - row_mean * row_mean
    inverse = lax.rsqrt(row_var + 1e-06)

    load_w.wait()
    step = 4

    def project(j, acc):
        v = gath[pl.ds(j * step, step)].astype(F32).reshape(step * feats, ROWS)
        rows = pl.ds(pl.multiple_of(j * (step * feats), step * feats), step * feats)
        low = ((v - row_mean) * inverse * gb_ref[rows, :]).astype(BF16)
        nt[pl.ds(j * step, step)] = low.reshape(step, feats, ROWS)
        return acc + dot(low, w_ref[rows, :], 0, 0)

    projected = lax.fori_loop(
        0, n_mp // step, project, jnp.zeros((ROWS, 3 * HEAD), F32)
    ).astype(BF16)

    mine = lax.rem(c + C * n_dp - d, C)

    def nt_copy(i, to):
        return rcopy(
            nt.at[to, pl.ds(pl.multiple_of(y * fy, fy), fy)],
            br.at[y, c, lax.div(d, C)],
            nt_s.at[i], nt_r.at[lax.div(d, C)], (to, m),
        )

    def nt_send(k, _):
        i = lax.rem(lax.div(d, C) + k, per_class)
        to = i * C + mine

        @pl.when(to != d)
        def _():
            nt_copy(i, to).start()

        return 0

    lax.fori_loop(0, per_class, nt_send, 0)

    @pl.when(mine == lax.rem(d, C))
    def _():
        br[y, c, lax.div(d, C)] = nt[d, pl.ds(pl.multiple_of(y * fy, fy), fy)]

    seg = jnp.broadcast_to(seg_ref[...].astype(F32), (ROWS, ROWS))
    attended, grads = head_pass(
        projected, qg_ref[...], kg_ref[...], seg == seg.T, cot_ref[...]
    )
    ga[d] = grads

    def z_copy(level, up):
        dev = (d + X, m) if up else (d - X, m)
        ref = ga.at[level * X + x]
        i = level + (ZL if up else 0)
        return rcopy(ref, ref, zg_s.at[i], zg_r.at[level], dev)

    def z_wait(level):
        ref = ga.at[level * X + x]
        dev = (lax.rem(d + X, n_dp), m)
        rcopy(ref, ref, zg_s.at[level], zg_r.at[level], dev).wait_recv()

    def gather_x(level):
        return Gather(
            ring_x,
            lambda q: ga.at[level * X + q],
            lambda q, i: ga.at[level * X + q, pl.ds(i * (ROWS // 2), ROWS // 2)],
            xg_s, xg_r, level * 4,
        )

    def levels(k, fn):
        @pl.when(z >= k)
        def _():
            fn(z - k, True)

        @pl.when(z + k < ZL)
        def _():
            fn(z + k, False)

    def z_step(level, below):
        z_wait(level)
        if below:

            @pl.when(z < ZL - 1)
            def _():
                z_copy(level, True).start()
        else:

            @pl.when(z > 0)
            def _():
                z_copy(level, False).start()

        gather_x(level).send()

    @pl.when(z < ZL - 1)
    def _():
        z_copy(z, True).start()

    @pl.when(z > 0)
    def _():
        z_copy(z, False).start()

    gather_x(z).send()
    attn_ref[...] = attended

    order = ring_h.others() + [h]

    def term(idx):
        hh = order[idx]
        rows = Y * C * feats
        block = dot(w_ref[pl.ds(pl.multiple_of(hh * rows, rows), rows), :], grads, 1, 1)
        block = block.astype(BF16)
        for q in range(Y):
            for core in range(C):
                at = (q * C + core) * feats
                ts[hh, core, q] = block[at : at + feats]
        if C == 2:
            core_copy(idx).start()

    def core_copy(idx):
        return rcopy(ts.at[order[idx], other], cr.at[idx], ca_s.at[idx], ca_r.at[idx], twin)

    def scatter_y(idx):
        hh = order[idx]
        return Scatter(
            ring_y,
            lambda q: ts.at[hh, c, q],
            lambda q, i: ts.at[hh, c, q, pl.ds(i * (feats // 2), feats // 2)],
            [ya.at[idx], yb.at[idx], yl.at[idx], yr.at[idx]],
            yr_s, yr_r, idx * 4,
        )

    s_y = [scatter_y(i) for i in range(len(order))]
    s_h = Scatter(
        ring_h,
        lambda q: qb.at[q],
        lambda q, i: qb.at[q, pl.ds(i * (feats // 2), feats // 2)],
        [za, zb, zl_, zr_],
        hr_s, hr_r, 0,
    )

    def rs_a(idx):
        if C == 2:
            core_copy(idx).wait_recv()
            add_to(ts.at[order[idx], c], cr.at[idx])
        s_y[idx].first()

    def rs_b(idx):
        s_y[idx].second()

    def rs_c(idx):
        qb[order[idx]] = s_y[idx].total().astype(BF16)

    for i in range(len(order)):
        term(i)

    g_n = Gather(
        ring_y,
        lambda q: br.at[q, c],
        lambda q, i: br.at[q, c, pl.ds(i * (per_class // 2), per_class // 2)],
        ny_s, ny_r, 0,
    )

    def n_copy(q, core):
        return rcopy(br.at[q, core], br.at[q, core], nc_s.at[q], nc_r.at[q], twin)

    def n_wait(k, _):
        i = lax.rem(lax.div(d, C) + per_class - k, per_class)

        @pl.when(i * C + mine != d)
        def _():
            rcopy(
                br.at[y, c, i], br.at[y, c, i], nt_s.at[i], nt_r.at[i], (lax.rem(d + 1, n_dp), m)
            ).wait_recv()

        return 0

    def n_to_twin(qs):
        if C == 2:
            for q in qs:
                n_copy(q, c).start()

    def n_first():
        lax.fori_loop(0, per_class, n_wait, 0)
        g_n.send()
        n_to_twin([y])

    def n_second():
        g_n.relay()
        n_to_twin(near_y)

    def n_third():
        g_n.last()
        n_to_twin(far_y)

    def n_last():
        if C == 2:
            for q in range(Y):
                n_copy(q, other).wait_recv()

    every = range(len(order))
    jobs = [
        [functools.partial(rs_a, i) for i in every] + [n_first],
        [functools.partial(rs_b, i) for i in every],
        [functools.partial(rs_c, i) for i in every] + [s_h.first, n_second],
        [s_h.second, n_third],
        [n_last],
    ]
    jobs = jobs + [[]] * (ZL - 1 - len(jobs))
    span = max(ZL - 1, 1)
    for k in range(1, ZL):
        levels(k, z_step)
        share = jobs[(k - 1) * len(jobs) // span : k * len(jobs) // span]
        for group in share:
            for job in group:
                job()
        if k == 1:
            gather_x(z).relay()
        else:
            levels(k - 1, lambda level, _: gather_x(level).relay())
    if ZL == 1:
        for group in jobs:
            for job in group:
                job()
        gather_x(z).relay()
    else:
        levels(ZL - 1, lambda level, _: gather_x(level).relay())

    wg_ref[...] = jnp.zeros_like(wg_ref)

    def weight_term(level):
        gather_x(level).last()
        left = []
        for q in range(X):
            src = level * X + q
            kind = lax.rem(d + src, C)
            left.append(br[:, kind, lax.div(src, C)].reshape(feats, ROWS))
        right = ga[pl.ds(level * X, X)].reshape(X * ROWS, 3 * HEAD)
        wg_ref[...] += dot(jnp.concatenate(left, axis=1), right, 1, 0)

    weight_term(z)

    def weight_step(k, _):
        levels(k, lambda level, _: weight_term(level))
        return 0

    lax.fori_loop(1, ZL, weight_step, 0)
    ng_ref[...] = s_h.total()

    def a2a_drain(k, _):
        to = lax.rem(d + k, n_dp)
        rcopy(out_buf.at[to], arr.at[d], a2a_s.at[to], a2a_r.at[d], (to, m)).wait_send()
        return 0

    lax.fori_loop(1, n_dp, a2a_drain, 0)
    g_h.drain()
    for g in g_y:
        g.drain()
    if C == 2:
        for i, hh in enumerate(come):
            for q in range(Y):
                twin_copy(i, hh, q, c).wait_send()

    def nt_drain(i, _):
        @pl.when(i * C + mine != d)
        def _():
            nt_copy(i, i * C + mine).wait_send()

        return 0

    lax.fori_loop(0, per_class, nt_drain, 0)
    g_n.drain()
    if C == 2:
        for q in range(Y):
            n_copy(q, c).wait_send()
        for i in every:
            core_copy(i).wait_send()
    for i in every:
        s_y[i].drain()
    s_h.drain()

    @pl.when(z < ZL - 1)
    def _():
        z_copy(z, True).wait_send()

    @pl.when(z > 0)
    def _():
        z_copy(z, False).wait_send()

    gather_x(z).drain()

    def far_drain(level, below):
        @pl.when((z < ZL - 1) if below else (z > 0))
        def _():
            z_copy(level, below).wait_send()

        gather_x(level).drain()

    def z_drain(k, _):
        levels(k, far_drain)
        return 0

    lax.fori_loop(1, ZL, z_drain, 0)


def on_device(
    patches, route_owner, route_slot, segment_ids, ln_gain, qkv_weight, q_gain, k_gain, d_attn
):
    n_dp, n_mp = ZL * X, ZH * Y * C
    feats = patches.shape[1]
    width = qkv_weight.shape[0]
    ext = -(-(feats + 1) // 128) * 128
    vmem = pl.BlockSpec(memory_space=pltpu.VMEM)
    dma = lambda n: pltpu.SemaphoreType.DMA((max(n, 1),))
    half = feats // 2
    pairs = []
    for n in (n_dp, 4, 4 * ZH, ZH * Y, n_dp // C, 4, Y):
        pairs += [dma(n), dma(n)]
    pairs += [dma(2 * ZL), dma(ZL), dma(4 * ZL), dma(4 * ZL)]
    for n in (ZH, 4 * ZH, 4):
        pairs += [dma(n), dma(n)]
    return pl.pallas_call(
        kernel,
        out_shape=(
            jax.ShapeDtypeStruct((ROWS, HEAD), BF16),
            jax.ShapeDtypeStruct((feats, ROWS), F32),
            jax.ShapeDtypeStruct((width // n_dp, 3 * HEAD), F32),
        ),
        in_specs=[vmem] * 5 + [pl.BlockSpec(memory_space=pl.ANY)] + [vmem] * 3,
        out_specs=(vmem, vmem, vmem),
        scratch_shapes=[
            pltpu.VMEM((width, 3 * HEAD), BF16),
            pltpu.VMEM((width, 128), F32),
            pltpu.VMEM((ext, ROWS), BF16),
            pltpu.VMEM((n_dp, SLOT, ext), BF16),
            pltpu.VMEM((n_dp, SLOT, ext), BF16),
            pltpu.VMEM((n_mp, feats, ROWS), BF16),
            pltpu.VMEM((n_mp, feats, ROWS), BF16),
            pltpu.VMEM((Y, C, n_dp // C, feats // Y, ROWS), BF16),
            pltpu.VMEM((n_dp, ROWS, 3 * HEAD), BF16),
            pltpu.VMEM((ZH, C, Y, feats, ROWS), BF16),
            pltpu.VMEM((ZH, Y, feats, ROWS), BF16),
            pltpu.VMEM((ZH, half, ROWS), BF16),
            pltpu.VMEM((ZH, half, ROWS), BF16),
            pltpu.VMEM((ZH, feats, ROWS), BF16),
            pltpu.VMEM((ZH, feats, ROWS), BF16),
            pltpu.VMEM((ZH, feats, ROWS), BF16),
            pltpu.VMEM((half, ROWS), BF16),
            pltpu.VMEM((half, ROWS), BF16),
            pltpu.VMEM((feats, ROWS), BF16),
            pltpu.VMEM((feats, ROWS), BF16),
            pltpu.SemaphoreType.DMA,
            *pairs,
        ],
        compiler_params=pltpu.CompilerParams(
            collective_id=0, has_side_effects=True, vmem_limit_bytes=48 * 1024 * 1024
        ),
    )(
        patches.T,
        route_owner.reshape(1, ROWS),
        route_slot.reshape(1, ROWS),
        segment_ids,
        ln_gain.reshape(width // 128, 128),
        qkv_weight,
        q_gain.reshape(1, HEAD),
        k_gain.reshape(1, HEAD),
        d_attn,
    )


def solution(mesh):
    in_specs = (
        P("dp", "mp"),
        P("dp"),
        P("dp"),
        P("dp", None),
        P(),
        P(None, "mp"),
        P("mp"),
        P("mp"),
        P("dp", "mp"),
    )
    out_specs = (P("dp", "mp"), P("mp", "dp"), P("dp", "mp"))
    return jax.shard_map(
        on_device, mesh=mesh, in_specs=in_specs, out_specs=out_specs, check_vma=False
    )
```

```python
import functools
import math

import jax
import jax.numpy as jnp
from jax import lax
from jax.experimental import pallas as pl
from jax.experimental.pallas import tpu as pltpu
from jax.sharding import PartitionSpec as P

MESH = pl.DeviceIdType.MESH
F32 = jnp.float32
BF16 = jnp.bfloat16
HEAD = 128
ROWS = 128
ZL, X = 8, 4
ZH, Y, C = 4, 4, 2
EXPRESS = 4
SLOT = 16
HIGHEST = lax.Precision.HIGHEST


def dot(a, b, ca, cb, precision=None):
    return lax.dot_general(
        a, b, (((ca,), (cb,)), ((), ())), precision=precision, preferred_element_type=F32
    )


def rcopy(src, dst, ssem, rsem, dev):
    return pltpu.make_async_remote_copy(
        src_ref=src, dst_ref=dst, send_sem=ssem, recv_sem=rsem, device_id=dev, device_id_type=MESH
    )


class Ring:
    def __init__(self, n, p, dev):
        self.n, self.p = n, p
        self.right = lax.rem(p + 1, n)
        self.left = lax.rem(p + n - 1, n)
        self.opp = lax.rem(p + 2, n)
        self.dev_right, self.dev_left = dev(self.right), dev(self.left)

    def others(self):
        return {1: [], 2: [self.left], 4: [self.opp, self.left, self.right]}[self.n]

    def neighbours(self):
        return {1: [], 2: [self.dev_right], 4: [self.dev_left, self.dev_right]}[self.n]


class Gather:
    SENDS = 6

    def __init__(self, ring, block, half, ss, rs, base):
        self.ring, self.block, self.half = ring, block, half
        self.ss, self.rs, self.base = ss, rs, base * self.SENDS

    def _copy(self, ref, i, dev):
        return rcopy(ref, ref, self.ss.at[self.base + i], self.rs.at[self.base + i], dev)

    def _sent(self):
        g = self.ring
        if g.n == 1:
            return []
        if g.n == 2:
            return [lambda: self._copy(self.block(g.p), 0, g.dev_right)]
        return [
            lambda: self._copy(self.half(g.p, 0), 0, g.dev_right),
            lambda: self._copy(self.half(g.p, 1), 1, g.dev_left),
            lambda: self._copy(self.half(g.p, 1), 2, g.dev_right),
            lambda: self._copy(self.half(g.p, 0), 3, g.dev_left),
            lambda: self._copy(self.half(g.left, 0), 4, g.dev_right),
            lambda: self._copy(self.half(g.right, 1), 5, g.dev_left),
        ]

    def send(self):
        for copy in self._sent()[:4]:
            copy().start()

    def relay(self):
        g = self.ring
        if g.n == 4:
            sent = self._sent()
            self._copy(self.half(g.left, 0), 0, g.dev_right).wait_recv()
            sent[4]().start()
            self._copy(self.half(g.right, 1), 1, g.dev_left).wait_recv()
            sent[5]().start()

    def rest(self):
        g = self.ring
        if g.n == 2:
            self._copy(self.block(g.left), 0, g.dev_right).wait_recv()
        if g.n == 4:
            self._copy(self.half(g.left, 1), 2, g.dev_right).wait_recv()
            self._copy(self.half(g.right, 0), 3, g.dev_left).wait_recv()

    def last(self):
        g = self.ring
        if g.n == 4:
            self._copy(self.half(g.opp, 0), 4, g.dev_right).wait_recv()
            self._copy(self.half(g.opp, 1), 5, g.dev_left).wait_recv()

    def drain(self):
        for copy in self._sent():
            copy().wait_send()


class Scatter:
    SENDS = 6

    def __init__(self, ring, block, half, bufs, ss, rs, base):
        self.ring, self.block, self.half, self.bufs = ring, block, half, bufs
        self.ss, self.rs, self.base = ss, rs, base * self.SENDS

    def _copy(self, ref, dst, i, dev):
        return rcopy(ref, dst, self.ss.at[self.base + i], self.rs.at[self.base + i], dev)

    def _sent(self):
        g, b = self.ring, self.bufs
        if g.n == 1:
            return []
        if g.n == 2:
            return [lambda: self._copy(self.block(g.right), b[2], 0, g.dev_right)]
        return [
            lambda: self._copy(self.half(g.opp, 0), b[0], 0, g.dev_right),
            lambda: self._copy(self.half(g.opp, 1), b[1], 1, g.dev_left),
            lambda: self._copy(self.half(g.right, 1), self._part(b[2], 1), 2, g.dev_right),
            lambda: self._copy(self.half(g.left, 0), self._part(b[3], 0), 3, g.dev_left),
            lambda: self._copy(self.half(g.right, 0), self._part(b[2], 0), 4, g.dev_right),
            lambda: self._copy(self.half(g.left, 1), self._part(b[3], 1), 5, g.dev_left),
        ]

    @staticmethod
    def _part(ref, i):
        rows = ref.shape[0] // 2
        return ref.at[pl.ds(i * rows, rows)]

    def first(self):
        for copy in self._sent()[:4]:
            copy().start()

    def second(self):
        g = self.ring
        if g.n == 4:
            sent = self._sent()
            sent[0]().wait_recv()
            add_to(self.half(g.right, 0), self.bufs[0])
            sent[4]().start()
            sent[1]().wait_recv()
            add_to(self.half(g.left, 1), self.bufs[1])
            sent[5]().start()

    def total(self):
        g, sent = self.ring, self._sent()
        out = self.block(g.p)[...].astype(F32)
        if g.n == 2:
            sent[0]().wait_recv()
        if g.n == 4:
            for i in (2, 3, 4, 5):
                sent[i]().wait_recv()
        if g.n > 1:
            out = out + self.bufs[2][...].astype(F32)
        if g.n == 4:
            out = out + self.bufs[3][...].astype(F32)
        return out

    def drain(self):
        for copy in self._sent():
            copy().wait_send()


def add_to(ref, other):
    ref[...] = (ref[...].astype(F32) + other[...].astype(F32)).astype(ref.dtype)


def mean_of(v):
    return jnp.mean(v, axis=1, keepdims=True)


def norm_head(vector, gain_row):
    center = vector - mean_of(vector)
    inverse = lax.rsqrt(mean_of(center * center) + 1e-06)
    unit_rows = center * inverse
    return unit_rows * gain_row, unit_rows, inverse


def norm_head_back(cotangent, unit_rows, inverse, gain_row):
    scaled = cotangent * gain_row
    return inverse * (scaled - mean_of(scaled) - unit_rows * mean_of(scaled * unit_rows))


def head_pass(projected, gain_query, gain_key, allowed, cotangent):
    value_rows = projected[:, 2 * HEAD :]
    query_n, query_u, query_r = norm_head(projected[:, :HEAD].astype(F32), gain_query)
    key_n, key_u, key_r = norm_head(projected[:, HEAD : 2 * HEAD].astype(F32), gain_key)
    factor = 1.0 / math.sqrt(HEAD)
    scores = dot(query_n, key_n, 1, 1, HIGHEST) * factor
    scores = jnp.where(allowed, scores, -1e30)
    shifted = jnp.exp(scores - jnp.max(scores, axis=1, keepdims=True))
    softmax_rows = shifted / jnp.sum(shifted, axis=1, keepdims=True)
    probs_low = softmax_rows.astype(BF16)
    attended = dot(probs_low, value_rows, 1, 0).astype(BF16)
    grad_value = dot(probs_low, cotangent, 0, 0)
    grad_probs = dot(cotangent, value_rows, 1, 1)
    grad_scores = softmax_rows * (
        grad_probs - jnp.sum(grad_probs * softmax_rows, axis=1, keepdims=True)
    )
    grad_qn = dot(grad_scores, key_n, 1, 0, HIGHEST) * factor
    grad_kn = dot(grad_scores, query_n, 0, 0, HIGHEST) * factor
    grad_query = norm_head_back(grad_qn, query_u, query_r, gain_query)
    grad_key = norm_head_back(grad_kn, key_u, key_r, gain_key)
    return attended, jnp.concatenate([grad_query, grad_key, grad_value], axis=1).astype(BF16)


def kernel(
    patches_hbm, owner_hbm, slot_hbm, seg_hbm, gain_hbm, w_hbm, qg_hbm, kg_hbm, cot_hbm,
    attn_ref, ng_ref, wg_ref,
    patches_ref, owner_ref, slot_ref, seg_ref, gain_ref, w_ref, qg_ref, kg_ref, cot_ref,
    gb_ref, pt_ref, out_buf, arr, gath, nt, br, ga, ts, cr, ya, yb, yl, yr, qb, za, zb, zl_, zr_,
    wa, wb, xa, xb, xl, xr,
    in_sem, a2a_s, a2a_r, hg_s, hg_r, yg_s, yg_r, cg_s, cg_r, nt_s, nt_r, ny_s, ny_r, nc_s, nc_r,
    zg_s, zg_r, xs_s, xs_r, ca_s, ca_r, yr_s, yr_r, hr_s, hr_r,
):
    n_dp, n_mp = ZL * X, ZH * Y * C
    feats = patches_hbm.shape[0]
    width = n_mp * feats
    fy = feats // Y
    per_class = ZL // C
    d, m = lax.axis_index("dp"), lax.axis_index("mp")
    z, x = lax.div(d, X), lax.rem(d, X)
    h, y, c = lax.div(m, Y * C), lax.rem(lax.div(m, C), Y), lax.rem(m, C)
    ring_h = Ring(ZH, h, lambda q: (d, (q * Y + y) * C + c))
    ring_y = Ring(Y, y, lambda q: (d, (h * Y + q) * C + c))
    ring_x = Ring(X, x, lambda q: (z * X + q, m))
    twin = (d, (h * Y + y) * C + (1 - c))
    other = 1 - c

    loads = [
        pltpu.make_async_copy(src, dst, in_sem.at[i])
        for i, (src, dst) in enumerate([
            (owner_hbm, owner_ref), (patches_hbm, patches_ref), (slot_hbm, slot_ref),
            (gain_hbm, gain_ref), (seg_hbm, seg_ref), (qg_hbm, qg_ref), (kg_hbm, kg_ref),
            (cot_hbm, cot_ref), (w_hbm, w_ref),
        ])
    ]
    for load in loads:
        load.start()

    barrier = pltpu.get_barrier_semaphore()

    def hail(k, _):
        to = lax.rem(d + k, n_dp)
        pl.semaphore_signal(barrier, inc=1, device_id=(to, m), device_id_type=MESH)
        return 0

    lax.fori_loop(1, n_dp, hail, 0)
    near = ring_h.neighbours() + ring_y.neighbours() + ([twin] if C == 2 else [])
    for dev in near:
        pl.semaphore_signal(barrier, inc=1, device_id=dev, device_id_type=MESH)

    for load in loads[:4]:
        load.wait()
    owners = jnp.broadcast_to(owner_ref[...].astype(F32), (ROWS, ROWS))
    rows_i = lax.broadcasted_iota(jnp.int32, (ROWS, ROWS), 0)
    cols_i = lax.broadcasted_iota(jnp.int32, (ROWS, ROWS), 1)
    same = jnp.where((owners == owners.T) & (rows_i < cols_i), 1.0, 0.0)
    rank = jnp.sum(same, axis=0, keepdims=True)
    target = owner_ref[...].astype(F32) * SLOT + rank
    slots_i = lax.broadcasted_iota(jnp.int32, (n_dp * SLOT, ROWS), 0).astype(F32)
    pick = jnp.where(slots_i == target, 1.0, 0.0).astype(BF16)
    pt_ref[:feats] = patches_ref[...]
    pt_ref[feats:] = jnp.broadcast_to(
        slot_ref[...].astype(F32) + 1.0, (pt_ref.shape[0] - feats, ROWS)
    ).astype(BF16)
    outgoing = dot(pick, pt_ref[...], 1, 1).astype(BF16)
    out_buf[...] = outgoing.reshape(out_buf.shape)

    pl.semaphore_wait(barrier, n_dp - 1 + len(near))

    def a2a_send(k, _):
        to = lax.rem(d + k, n_dp)
        rcopy(out_buf.at[to], arr.at[d], a2a_s.at[to], a2a_r.at[d], (to, m)).start()
        return 0

    lax.fori_loop(1, n_dp, a2a_send, 0)
    arr[d] = out_buf[d]

    def spread_gain(j, _):
        tile = jnp.broadcast_to(gain_ref[pl.ds(j, 1), :], (128, 128))
        gb_ref[pl.ds(pl.multiple_of(j * 128, 128), 128), :] = tile.T
        return 0

    lax.fori_loop(0, width // 128, spread_gain, 0)

    def a2a_wait(k, _):
        frm = lax.rem(d + n_dp - k, n_dp)
        rcopy(out_buf.at[frm], arr.at[frm], a2a_s.at[frm], a2a_r.at[frm], (frm, m)).wait_recv()
        return 0

    lax.fori_loop(1, n_dp, a2a_wait, 0)
    arrived = arr[...].reshape(n_dp * SLOT, arr.shape[2])
    lanes = lax.broadcasted_iota(jnp.int32, (n_dp * SLOT, ROWS), 1).astype(F32) + 1.0
    place = jnp.where(
        lanes == arrived[:, feats : feats + 1].astype(F32), 1.0, 0.0
    ).astype(BF16)
    gath[m] = dot(arrived[:, :feats], place, 0, 0).astype(BF16)

    g_h = Gather(
        ring_h,
        lambda q: gath.at[(q * Y + y) * C + c],
        lambda q, i: gath.at[(q * Y + y) * C + c, pl.ds(i * (feats // 2), feats // 2)],
        hg_s, hg_r, 0,
    )

    def gather_y(idx, hh):
        return Gather(
            ring_y,
            lambda q: gath.at[(hh * Y + q) * C + c],
            lambda q, i: gath.at[(hh * Y + q) * C + c, pl.ds(i * (feats // 2), feats // 2)],
            yg_s, yg_r, idx,
        )

    def twin_copy(idx, hh, q, core):
        ref = gath.at[(hh * Y + q) * C + core]
        i = idx * Y + q
        return rcopy(ref, ref, cg_s.at[i], cg_r.at[i], twin)

    def to_twin(idx, hh, qs):
        if C == 2:
            for q in qs:
                twin_copy(idx, hh, q, c).start()

    come = [h] + {1: [], 2: [ring_h.left], 4: [ring_h.left, ring_h.right, ring_h.opp]}[ZH]
    g_y = [gather_y(i, hh) for i, hh in enumerate(come)]
    near_y = {1: [], 2: [ring_y.left], 4: [ring_y.left, ring_y.right]}[Y]
    far_y = [ring_y.opp] if Y == 4 else []

    def own_y(i):
        g_y[i].send()
        to_twin(i, come[i], [y])

    def next_y(i):
        g_y[i].relay()
        g_y[i].rest()
        to_twin(i, come[i], near_y)

    def last_y(i):
        g_y[i].last()
        to_twin(i, come[i], far_y)

    g_h.send()
    own_y(0)
    next_y(0)
    g_h.relay()
    last_y(0)
    g_h.rest()
    near_h = range(1, min(len(come), 3))
    for i in near_h:
        own_y(i)
    for i in near_h:
        next_y(i)
    for i in near_h:
        last_y(i)
    g_h.last()
    if ZH == 4:
        own_y(3)
        next_y(3)
        last_y(3)
    if C == 2:
        for i, hh in enumerate(come):
            for q in range(Y):
                twin_copy(i, hh, q, other).wait_recv()

    def sums(j, carry):
        s1, s2 = carry
        v = gath[j].astype(F32).reshape(feats // 8, 8, ROWS)
        return s1 + jnp.sum(v, axis=0), s2 + jnp.sum(v * v, axis=0)

    zero = jnp.zeros((8, ROWS), F32)
    s1, s2 = lax.fori_loop(0, n_mp, sums, (zero, zero))
    row_mean = jnp.sum(s1, axis=0, keepdims=True) / width
    row_var = jnp.sum(s2, axis=0, keepdims=True) / width - row_mean * row_mean
    inverse = lax.rsqrt(row_var + 1e-06)

    for load in loads[4:]:
        load.wait()
    step = 4

    def project(j, acc):
        v = gath[pl.ds(j * step, step)].astype(F32).reshape(step * feats, ROWS)
        rows = pl.ds(pl.multiple_of(j * (step * feats), step * feats), step * feats)
        low = ((v - row_mean) * inverse * gb_ref[rows, :]).astype(BF16)
        nt[pl.ds(j * step, step)] = low.reshape(step, feats, ROWS)
        return acc + dot(low, w_ref[rows, :], 0, 0)

    projected = lax.fori_loop(
        0, n_mp // step, project, jnp.zeros((ROWS, 3 * HEAD), F32)
    ).astype(BF16)

    mine = lax.rem(c + C * ZL - z, C)
    share = pl.ds(pl.multiple_of(y * fy, fy), fy)

    def nt_copy(i):
        to = i * C + mine
        return rcopy(
            nt.at[pl.ds(to * X, X), share], br.at[y, c, lax.div(z, C)],
            nt_s.at[i], nt_r.at[lax.div(z, C)], (to * X + x, m),
        )

    def partners(fn):
        def one(i, _):
            @pl.when(i * C + mine != z)
            def _():
                fn(i)

            return 0

        lax.fori_loop(0, per_class, one, 0)

    partners(lambda i: nt_copy(i).start())

    @pl.when(mine == lax.rem(z, C))
    def _():
        br[y, c, lax.div(z, C)] = nt[pl.ds(z * X, X), share]

    seg = jnp.broadcast_to(seg_ref[...].astype(F32), (ROWS, ROWS))
    attended, grads = head_pass(
        projected, qg_ref[...], kg_ref[...], seg == seg.T, cot_ref[...]
    )
    ga[z] = grads

    def z_half(level, i):
        return ga.at[level, pl.ds(i * (ROWS // 2), ROWS // 2)]

    def z_copy(level, up, i, far=False):
        step = X * EXPRESS if far else X
        dev = (d + step, m) if up else (d - step, m)
        at = level * 2 + i
        ref = z_half(level, i)
        out = at + (2 * ZL if up else 0) + (4 * ZL if far else 0)
        return rcopy(ref, ref, zg_s.at[out], zg_r.at[at], dev)

    def z_wait(level, i):
        ref = z_half(level, i)
        at = level * 2 + i
        rcopy(ref, ref, zg_s.at[at], zg_r.at[at], (lax.rem(d + X, n_dp), m)).wait_recv()

    def levels(k, fn):
        @pl.when(z >= k)
        def _():
            fn(z - k, True)

        @pl.when(z + k < ZL)
        def _():
            fn(z + k, False)

    def z_on(level, below, k, fn):
        for up in (True, False):
            if k == 0 or (below == up and k % EXPRESS != EXPRESS - 1):

                @pl.when((z < ZL - 1) if up else (z > 0))
                def _():
                    fn(level, up, False)

            if k == 0 and EXPRESS < ZL:

                @pl.when((z + EXPRESS < ZL) if up else (z >= EXPRESS))
                def _():
                    fn(level, up, True)

    def z_step(k, i):
        def one(level, below):
            z_wait(level, i)
            z_on(level, below, k, lambda level, up, far: z_copy(level, up, i, far).start())

        return one

    for i in (0, 1):
        z_on(z, None, 0, lambda level, up, far: z_copy(level, up, i, far).start())
    attn_ref[...] = attended

    order = ring_h.others() + [h]

    def term(idx):
        hh = order[idx]
        rows = Y * C * feats
        block = dot(w_ref[pl.ds(pl.multiple_of(hh * rows, rows), rows), :], grads, 1, 1)
        block = block.astype(BF16)
        for q in range(Y):
            for core in range(C):
                at = (q * C + core) * feats
                ts[hh, core, q] = block[at : at + feats]
        if C == 2:
            core_copy(idx).start()

    def core_copy(idx):
        return rcopy(ts.at[order[idx], other], cr.at[idx], ca_s.at[idx], ca_r.at[idx], twin)

    def scatter_y(idx):
        hh = order[idx]
        return Scatter(
            ring_y,
            lambda q: ts.at[hh, c, q],
            lambda q, i: ts.at[hh, c, q, pl.ds(i * (feats // 2), feats // 2)],
            [ya.at[idx], yb.at[idx], yl.at[idx], yr.at[idx]],
            yr_s, yr_r, idx,
        )

    s_y = [scatter_y(i) for i in range(len(order))]
    s_h = Scatter(
        ring_h,
        lambda q: qb.at[q],
        lambda q, i: qb.at[q, pl.ds(i * (feats // 2), feats // 2)],
        [za, zb, zl_, zr_],
        hr_s, hr_r, 0,
    )

    def rs_a(idx):
        if C == 2:
            core_copy(idx).wait_recv()
            add_to(ts.at[order[idx], c], cr.at[idx])
        s_y[idx].first()

    def rs_b(idx):
        s_y[idx].second()

    def rs_c(idx):
        qb[order[idx]] = s_y[idx].total().astype(BF16)

    for i in range(len(order)):
        term(i)

    g_n = Gather(
        ring_y,
        lambda q: br.at[q, c],
        lambda q, i: br.at[q, c, pl.ds(i * (per_class // 2), per_class // 2)],
        ny_s, ny_r, 0,
    )

    def n_copy(q, core):
        return rcopy(br.at[q, core], br.at[q, core], nc_s.at[q], nc_r.at[q], twin)

    def n_wait(i):
        ref = br.at[y, c, i]
        rcopy(ref, ref, nt_s.at[i], nt_r.at[i], (lax.rem(d + X, n_dp), m)).wait_recv()

    def n_to_twin(qs):
        if C == 2:
            for q in qs:
                n_copy(q, c).start()

    def n_first():
        partners(n_wait)
        g_n.send()
        n_to_twin([y])

    def n_second():
        g_n.relay()
        g_n.rest()
        n_to_twin(near_y)

    def n_third():
        g_n.last()
        n_to_twin(far_y)

    def n_last():
        if C == 2:
            for q in range(Y):
                n_copy(q, other).wait_recv()

    every = range(len(order))
    jobs = [
        [functools.partial(rs_a, i) for i in every] + [n_first],
        [functools.partial(rs_b, i) for i in every] + [n_second],
        [functools.partial(rs_c, i) for i in every] + [s_h.first, n_third],
        [n_last],
        [],
        [],
        [s_h.second],
    ]

    def weight_term(level, _=None):
        kind, i = lax.rem(z + level, C), lax.div(level, C)
        left = [br[:, kind, i, q].reshape(feats, ROWS) for q in range(X)]
        wa[...] += dot(jnp.concatenate(left, axis=0), ga[level], 1, 0)

    away = sorted(range(1, ZL), key=lambda k: (k // EXPRESS + k % EXPRESS, k))

    def weight_terms(first, last):
        def one(at, _):
            k = at + 1
            for i, value in enumerate(away):
                k = jnp.where(at == i, value, k)
            levels(k, weight_term)
            return 0

        lax.fori_loop(first, last, one, 0)

    wa[...] = jnp.zeros_like(wa)
    for at in range(max(len(away), len(jobs))):
        if at < len(away):
            levels(away[at], z_step(away[at], 0))
            levels(away[at], z_step(away[at], 1))
        for job in jobs[at] if at < len(jobs) else []:
            job()
        if at == 4:
            weight_term(z)
            weight_terms(0, min(at, len(away)))
    weight_terms(min(4, len(away)), len(away))
    wb[...] = wa[...].astype(BF16).reshape(wb.shape)
    s_x = Scatter(
        ring_x,
        lambda q: wb.at[q],
        lambda q, i: wb.at[q, pl.ds(i * (feats // 2), feats // 2)],
        [xa, xb, xl, xr],
        xs_s, xs_r, 0,
    )
    s_x.first()
    s_x.second()
    wg_ref[...] = s_x.total()
    ng_ref[...] = s_h.total()

    def a2a_drain(k, _):
        to = lax.rem(d + k, n_dp)
        rcopy(out_buf.at[to], arr.at[d], a2a_s.at[to], a2a_r.at[d], (to, m)).wait_send()
        return 0

    lax.fori_loop(1, n_dp, a2a_drain, 0)
    g_h.drain()
    for g in g_y:
        g.drain()
    if C == 2:
        for i, hh in enumerate(come):
            for q in range(Y):
                twin_copy(i, hh, q, c).wait_send()

    partners(lambda i: nt_copy(i).wait_send())
    g_n.drain()
    if C == 2:
        for q in range(Y):
            n_copy(q, c).wait_send()
        for i in every:
            core_copy(i).wait_send()
    for i in every:
        s_y[i].drain()
    s_h.drain()

    def z_sent(level, up, far):
        for i in (0, 1):
            z_copy(level, up, i, far).wait_send()

    z_on(z, None, 0, z_sent)
    for k in away:
        levels(k, lambda level, below: z_on(level, below, k, z_sent))
    s_x.drain()


def on_device(
    patches, route_owner, route_slot, segment_ids, ln_gain, qkv_weight, q_gain, k_gain, d_attn
):
    n_dp, n_mp = ZL * X, ZH * Y * C
    feats = patches.shape[1]
    width = qkv_weight.shape[0]
    ext = -(-(feats + 1) // 128) * 128
    vmem = pl.BlockSpec(memory_space=pltpu.VMEM)
    dma = lambda n: pltpu.SemaphoreType.DMA((max(n, 1),))
    half = feats // 2
    pairs = []
    for n in (n_dp, 6, 6 * ZH, ZH * Y, ZL // C, 6, Y):
        pairs += [dma(n), dma(n)]
    pairs += [dma(8 * ZL), dma(2 * ZL), dma(6), dma(6)]
    for n in (ZH, 6 * ZH, 6):
        pairs += [dma(n), dma(n)]
    operands = (
        patches.T,
        route_owner.reshape(1, ROWS),
        route_slot.reshape(1, ROWS),
        segment_ids,
        ln_gain.reshape(width // 128, 128),
        qkv_weight,
        q_gain.reshape(1, HEAD),
        k_gain.reshape(1, HEAD),
        d_attn,
    )
    return pl.pallas_call(
        kernel,
        out_shape=(
            jax.ShapeDtypeStruct((ROWS, HEAD), BF16),
            jax.ShapeDtypeStruct((feats, ROWS), F32),
            jax.ShapeDtypeStruct((width // n_dp, 3 * HEAD), F32),
        ),
        in_specs=[pl.BlockSpec(memory_space=pl.ANY)] * 9,
        out_specs=(vmem, vmem, vmem),
        scratch_shapes=[
            *[pltpu.VMEM(a.shape, a.dtype) for a in operands],
            pltpu.VMEM((width, 128), F32),
            pltpu.VMEM((ext, ROWS), BF16),
            pltpu.VMEM((n_dp, SLOT, ext), BF16),
            pltpu.VMEM((n_dp, SLOT, ext), BF16),
            pltpu.VMEM((n_mp, feats, ROWS), BF16),
            pltpu.VMEM((n_mp, feats, ROWS), BF16),
            pltpu.VMEM((Y, C, ZL // C, X, feats // Y, ROWS), BF16),
            pltpu.VMEM((ZL, ROWS, 3 * HEAD), BF16),
            pltpu.VMEM((ZH, C, Y, feats, ROWS), BF16),
            pltpu.VMEM((ZH, Y, feats, ROWS), BF16),
            pltpu.VMEM((ZH, half, ROWS), BF16),
            pltpu.VMEM((ZH, half, ROWS), BF16),
            pltpu.VMEM((ZH, feats, ROWS), BF16),
            pltpu.VMEM((ZH, feats, ROWS), BF16),
            pltpu.VMEM((ZH, feats, ROWS), BF16),
            pltpu.VMEM((half, ROWS), BF16),
            pltpu.VMEM((half, ROWS), BF16),
            pltpu.VMEM((feats, ROWS), BF16),
            pltpu.VMEM((feats, ROWS), BF16),
            pltpu.VMEM((X * feats, 3 * HEAD), F32),
            pltpu.VMEM((X, feats, 3 * HEAD), BF16),
            pltpu.VMEM((half, 3 * HEAD), BF16),
            pltpu.VMEM((half, 3 * HEAD), BF16),
            pltpu.VMEM((feats, 3 * HEAD), BF16),
            pltpu.VMEM((feats, 3 * HEAD), BF16),
            dma(len(operands)),
            *pairs,
        ],
        compiler_params=pltpu.CompilerParams(
            collective_id=0, has_side_effects=True, vmem_limit_bytes=62 * 1024 * 1024
        ),
    )(*operands)


def solution(mesh):
    in_specs = (
        P("dp", "mp"),
        P("dp"),
        P("dp"),
        P("dp", None),
        P(),
        P(None, "mp"),
        P("mp"),
        P("mp"),
        P("dp", "mp"),
    )
    out_specs = (P("dp", "mp"), P("mp", "dp"), P("dp", "mp"))
    return jax.shard_map(
        on_device, mesh=mesh, in_specs=in_specs, out_specs=out_specs, check_vma=False
    )
```

```python
import functools
import math

import jax
import jax.numpy as jnp
from jax import lax
from jax.experimental import pallas as pl
from jax.experimental.pallas import tpu as pltpu
from jax.sharding import PartitionSpec as P

MESH = pl.DeviceIdType.MESH
F32 = jnp.float32
BF16 = jnp.bfloat16
HEAD = 128
ROWS = 128
ZL, X = 8, 4
ZH, Y, C = 4, 4, 2
EXPRESS = 4
SLOT = 16
HIGHEST = lax.Precision.HIGHEST


def dot(a, b, ca, cb, precision=None):
    return lax.dot_general(
        a, b, (((ca,), (cb,)), ((), ())), precision=precision, preferred_element_type=F32
    )


def rcopy(src, dst, ssem, rsem, dev):
    return pltpu.make_async_remote_copy(
        src_ref=src, dst_ref=dst, send_sem=ssem, recv_sem=rsem, device_id=dev, device_id_type=MESH
    )


class Ring:
    def __init__(self, n, p, dev):
        self.n, self.p = n, p
        self.right = lax.rem(p + 1, n)
        self.left = lax.rem(p + n - 1, n)
        self.opp = lax.rem(p + 2, n)
        self.dev_right, self.dev_left = dev(self.right), dev(self.left)

    def others(self):
        return {1: [], 2: [self.left], 4: [self.opp, self.left, self.right]}[self.n]

    def neighbours(self):
        return {1: [], 2: [self.dev_right], 4: [self.dev_left, self.dev_right]}[self.n]


class Gather:
    SENDS = 6

    def __init__(self, ring, block, half, ss, rs, base):
        self.ring, self.block, self.half = ring, block, half
        self.ss, self.rs, self.base = ss, rs, base * self.SENDS

    def _copy(self, ref, i, dev):
        return rcopy(ref, ref, self.ss.at[self.base + i], self.rs.at[self.base + i], dev)

    def _sent(self):
        g = self.ring
        if g.n == 1:
            return []
        if g.n == 2:
            return [lambda: self._copy(self.block(g.p), 0, g.dev_right)]
        return [
            lambda: self._copy(self.half(g.p, 0), 0, g.dev_right),
            lambda: self._copy(self.half(g.p, 1), 1, g.dev_left),
            lambda: self._copy(self.half(g.p, 1), 2, g.dev_right),
            lambda: self._copy(self.half(g.p, 0), 3, g.dev_left),
            lambda: self._copy(self.half(g.left, 0), 4, g.dev_right),
            lambda: self._copy(self.half(g.right, 1), 5, g.dev_left),
        ]

    def send(self):
        for copy in self._sent()[:4]:
            copy().start()

    def relay(self):
        g = self.ring
        if g.n == 4:
            sent = self._sent()
            self._copy(self.half(g.left, 0), 0, g.dev_right).wait_recv()
            sent[4]().start()
            self._copy(self.half(g.right, 1), 1, g.dev_left).wait_recv()
            sent[5]().start()

    def rest(self):
        g = self.ring
        if g.n == 2:
            self._copy(self.block(g.left), 0, g.dev_right).wait_recv()
        if g.n == 4:
            self._copy(self.half(g.left, 1), 2, g.dev_right).wait_recv()
            self._copy(self.half(g.right, 0), 3, g.dev_left).wait_recv()

    def last(self):
        g = self.ring
        if g.n == 4:
            self._copy(self.half(g.opp, 0), 4, g.dev_right).wait_recv()
            self._copy(self.half(g.opp, 1), 5, g.dev_left).wait_recv()

    def drain(self):
        for copy in self._sent():
            copy().wait_send()


class Scatter:
    SENDS = 6

    def __init__(self, ring, block, half, bufs, ss, rs, base):
        self.ring, self.block, self.half, self.bufs = ring, block, half, bufs
        self.ss, self.rs, self.base = ss, rs, base * self.SENDS

    def _copy(self, ref, dst, i, dev):
        return rcopy(ref, dst, self.ss.at[self.base + i], self.rs.at[self.base + i], dev)

    def _sent(self):
        g, b = self.ring, self.bufs
        if g.n == 1:
            return []
        if g.n == 2:
            return [lambda: self._copy(self.block(g.right), b[2], 0, g.dev_right)]
        return [
            lambda: self._copy(self.half(g.opp, 0), b[0], 0, g.dev_right),
            lambda: self._copy(self.half(g.opp, 1), b[1], 1, g.dev_left),
            lambda: self._copy(self.half(g.right, 1), self._part(b[2], 1), 2, g.dev_right),
            lambda: self._copy(self.half(g.left, 0), self._part(b[3], 0), 3, g.dev_left),
            lambda: self._copy(self.half(g.right, 0), self._part(b[2], 0), 4, g.dev_right),
            lambda: self._copy(self.half(g.left, 1), self._part(b[3], 1), 5, g.dev_left),
        ]

    @staticmethod
    def _part(ref, i):
        rows = ref.shape[0] // 2
        return ref.at[pl.ds(i * rows, rows)]

    def first(self):
        for copy in self._sent()[:4]:
            copy().start()

    def second(self):
        g = self.ring
        if g.n == 4:
            sent = self._sent()
            sent[0]().wait_recv()
            add_to(self.half(g.right, 0), self.bufs[0])
            sent[4]().start()
            sent[1]().wait_recv()
            add_to(self.half(g.left, 1), self.bufs[1])
            sent[5]().start()

    def total(self):
        g, sent = self.ring, self._sent()
        out = self.block(g.p)[...].astype(F32)
        if g.n == 2:
            sent[0]().wait_recv()
        if g.n == 4:
            for i in (2, 3, 4, 5):
                sent[i]().wait_recv()
        if g.n > 1:
            out = out + self.bufs[2][...].astype(F32)
        if g.n == 4:
            out = out + self.bufs[3][...].astype(F32)
        return out

    def drain(self):
        for copy in self._sent():
            copy().wait_send()


def add_to(ref, other):
    ref[...] = (ref[...].astype(F32) + other[...].astype(F32)).astype(ref.dtype)


def mean_of(v):
    return jnp.mean(v, axis=1, keepdims=True)


def norm_head(vector, gain_row):
    center = vector - mean_of(vector)
    inverse = lax.rsqrt(mean_of(center * center) + 1e-06)
    unit_rows = center * inverse
    return unit_rows * gain_row, unit_rows, inverse


def norm_head_back(cotangent, unit_rows, inverse, gain_row):
    scaled = cotangent * gain_row
    return inverse * (scaled - mean_of(scaled) - unit_rows * mean_of(scaled * unit_rows))


def head_pass(projected, gain_query, gain_key, allowed, cotangent):
    value_rows = projected[:, 2 * HEAD :]
    query_n, query_u, query_r = norm_head(projected[:, :HEAD].astype(F32), gain_query)
    key_n, key_u, key_r = norm_head(projected[:, HEAD : 2 * HEAD].astype(F32), gain_key)
    factor = 1.0 / math.sqrt(HEAD)
    scores = dot(query_n, key_n, 1, 1, HIGHEST) * factor
    scores = jnp.where(allowed, scores, -1e30)
    shifted = jnp.exp(scores - jnp.max(scores, axis=1, keepdims=True))
    softmax_rows = shifted / jnp.sum(shifted, axis=1, keepdims=True)
    probs_low = softmax_rows.astype(BF16)
    attended = dot(probs_low, value_rows, 1, 0).astype(BF16)
    grad_value = dot(probs_low, cotangent, 0, 0)
    grad_probs = dot(cotangent, value_rows, 1, 1)
    grad_scores = softmax_rows * (
        grad_probs - jnp.sum(grad_probs * softmax_rows, axis=1, keepdims=True)
    )
    grad_qn = dot(grad_scores, key_n, 1, 0, HIGHEST) * factor
    grad_kn = dot(grad_scores, query_n, 0, 0, HIGHEST) * factor
    grad_query = norm_head_back(grad_qn, query_u, query_r, gain_query)
    grad_key = norm_head_back(grad_kn, key_u, key_r, gain_key)
    return attended, jnp.concatenate([grad_query, grad_key, grad_value], axis=1).astype(BF16)


def kernel(
    patches_hbm, owner_hbm, slot_hbm, seg_hbm, gain_hbm, w_hbm, qg_hbm, kg_hbm, cot_hbm,
    attn_ref, ng_ref, wg_ref,
    patches_ref, owner_ref, slot_ref, seg_ref, gain_ref, w_ref, qg_ref, kg_ref, cot_ref,
    gb_ref, pt_ref, out_buf, arr, gath, nt, br, ga, ts, cr, ya, yb, yl, yr, qb, za, zb, zl_, zr_,
    wa, wb, xa, xb, xl, xr,
    in_sem, a2a_s, a2a_r, hg_s, hg_r, yg_s, yg_r, cg_s, cg_r, nt_s, nt_r, ny_s, ny_r, nc_s, nc_r,
    zg_s, zg_r, xs_s, xs_r, ca_s, ca_r, yr_s, yr_r, hr_s, hr_r,
):
    n_dp, n_mp = ZL * X, ZH * Y * C
    feats = patches_hbm.shape[0]
    width = n_mp * feats
    fy = feats // Y
    per_class = ZL // C
    d, m = lax.axis_index("dp"), lax.axis_index("mp")
    z, x = lax.div(d, X), lax.rem(d, X)
    h, y, c = lax.div(m, Y * C), lax.rem(lax.div(m, C), Y), lax.rem(m, C)
    ring_h = Ring(ZH, h, lambda q: (d, (q * Y + y) * C + c))
    ring_y = Ring(Y, y, lambda q: (d, (h * Y + q) * C + c))
    ring_x = Ring(X, x, lambda q: (z * X + q, m))
    twin = (d, (h * Y + y) * C + (1 - c))
    other = 1 - c

    loads = [
        pltpu.make_async_copy(src, dst, in_sem.at[i])
        for i, (src, dst) in enumerate([
            (owner_hbm, owner_ref), (patches_hbm, patches_ref), (slot_hbm, slot_ref),
            (gain_hbm, gain_ref), (seg_hbm, seg_ref), (qg_hbm, qg_ref), (kg_hbm, kg_ref),
            (cot_hbm, cot_ref), (w_hbm, w_ref),
        ])
    ]
    for load in loads:
        load.start()

    barrier = pltpu.get_barrier_semaphore()

    def hail(k, _):
        to = lax.rem(d + k, n_dp)
        pl.semaphore_signal(barrier, inc=1, device_id=(to, m), device_id_type=MESH)
        return 0

    lax.fori_loop(1, n_dp, hail, 0)
    near = ring_h.neighbours() + ring_y.neighbours() + ([twin] if C == 2 else [])
    for dev in near:
        pl.semaphore_signal(barrier, inc=1, device_id=dev, device_id_type=MESH)

    for load in loads[:4]:
        load.wait()
    owners = jnp.broadcast_to(owner_ref[...].astype(F32), (ROWS, ROWS))
    rows_i = lax.broadcasted_iota(jnp.int32, (ROWS, ROWS), 0)
    cols_i = lax.broadcasted_iota(jnp.int32, (ROWS, ROWS), 1)
    same = jnp.where((owners == owners.T) & (rows_i < cols_i), 1.0, 0.0)
    rank = jnp.sum(same, axis=0, keepdims=True)
    target = owner_ref[...].astype(F32) * SLOT + rank
    slots_i = lax.broadcasted_iota(jnp.int32, (n_dp * SLOT, ROWS), 0).astype(F32)
    pick = jnp.where(slots_i == target, 1.0, 0.0).astype(BF16)
    pt_ref[:feats] = patches_ref[...]
    pt_ref[feats:] = jnp.broadcast_to(
        slot_ref[...].astype(F32) + 1.0, (pt_ref.shape[0] - feats, ROWS)
    ).astype(BF16)
    outgoing = dot(pick, pt_ref[...], 1, 1).astype(BF16)
    out_buf[...] = outgoing.reshape(out_buf.shape)

    pl.semaphore_wait(barrier, n_dp - 1 + len(near))

    def a2a_send(k, _):
        to = lax.rem(d + k, n_dp)
        rcopy(out_buf.at[to], arr.at[d], a2a_s.at[to], a2a_r.at[d], (to, m)).start()
        return 0

    lax.fori_loop(1, n_dp, a2a_send, 0)
    arr[d] = out_buf[d]

    def spread_gain(j, _):
        tile = jnp.broadcast_to(gain_ref[pl.ds(j, 1), :], (128, 128))
        gb_ref[pl.ds(pl.multiple_of(j * 128, 128), 128), :] = tile.T
        return 0

    lax.fori_loop(0, width // 128, spread_gain, 0)

    def a2a_wait(k, _):
        frm = lax.rem(d + n_dp - k, n_dp)
        rcopy(out_buf.at[frm], arr.at[frm], a2a_s.at[frm], a2a_r.at[frm], (frm, m)).wait_recv()
        return 0

    lax.fori_loop(1, n_dp, a2a_wait, 0)
    arrived = arr[...].reshape(n_dp * SLOT, arr.shape[2])
    lanes = lax.broadcasted_iota(jnp.int32, (n_dp * SLOT, ROWS), 1).astype(F32) + 1.0
    place = jnp.where(
        lanes == arrived[:, feats : feats + 1].astype(F32), 1.0, 0.0
    ).astype(BF16)
    gath[m] = dot(arrived[:, :feats], place, 0, 0).astype(BF16)

    g_h = Gather(
        ring_h,
        lambda q: gath.at[(q * Y + y) * C + c],
        lambda q, i: gath.at[(q * Y + y) * C + c, pl.ds(i * (feats // 2), feats // 2)],
        hg_s, hg_r, 0,
    )

    def gather_y(idx, hh):
        return Gather(
            ring_y,
            lambda q: gath.at[(hh * Y + q) * C + c],
            lambda q, i: gath.at[(hh * Y + q) * C + c, pl.ds(i * (feats // 2), feats // 2)],
            yg_s, yg_r, idx,
        )

    def twin_copy(idx, hh, q, core):
        ref = gath.at[(hh * Y + q) * C + core]
        i = idx * Y + q
        return rcopy(ref, ref, cg_s.at[i], cg_r.at[i], twin)

    def to_twin(idx, hh, qs):
        if C == 2:
            for q in qs:
                twin_copy(idx, hh, q, c).start()

    come = [h] + {1: [], 2: [ring_h.left], 4: [ring_h.left, ring_h.right, ring_h.opp]}[ZH]
    g_y = [gather_y(i, hh) for i, hh in enumerate(come)]
    near_y = {1: [], 2: [ring_y.left], 4: [ring_y.left, ring_y.right]}[Y]
    far_y = [ring_y.opp] if Y == 4 else []

    def own_y(i):
        g_y[i].send()
        to_twin(i, come[i], [y])

    def next_y(i):
        g_y[i].relay()
        g_y[i].rest()
        to_twin(i, come[i], near_y)

    def last_y(i):
        g_y[i].last()
        to_twin(i, come[i], far_y)

    g_h.send()
    own_y(0)
    next_y(0)
    g_h.relay()
    last_y(0)
    g_h.rest()
    near_h = range(1, min(len(come), 3))
    for i in near_h:
        own_y(i)
    for i in near_h:
        next_y(i)
    for i in near_h:
        last_y(i)
    g_h.last()
    if ZH == 4:
        own_y(3)
        next_y(3)
        last_y(3)
    if C == 2:
        for i, hh in enumerate(come):
            for q in range(Y):
                twin_copy(i, hh, q, other).wait_recv()

    def sums(j, carry):
        s1, s2 = carry
        v = gath[j].astype(F32).reshape(feats // 8, 8, ROWS)
        return s1 + jnp.sum(v, axis=0), s2 + jnp.sum(v * v, axis=0)

    zero = jnp.zeros((8, ROWS), F32)
    s1, s2 = lax.fori_loop(0, n_mp, sums, (zero, zero))
    row_mean = jnp.sum(s1, axis=0, keepdims=True) / width
    row_var = jnp.sum(s2, axis=0, keepdims=True) / width - row_mean * row_mean
    inverse = lax.rsqrt(row_var + 1e-06)

    for load in loads[4:]:
        load.wait()
    step = 4

    def project(j, acc):
        v = gath[pl.ds(j * step, step)].astype(F32).reshape(step * feats, ROWS)
        rows = pl.ds(pl.multiple_of(j * (step * feats), step * feats), step * feats)
        low = ((v - row_mean) * inverse * gb_ref[rows, :]).astype(BF16)
        nt[pl.ds(j * step, step)] = low.reshape(step, feats, ROWS)
        return acc + dot(low, w_ref[rows, :], 0, 0)

    projected = lax.fori_loop(
        0, n_mp // step, project, jnp.zeros((ROWS, 3 * HEAD), F32)
    ).astype(BF16)

    mine = lax.rem(c + C * ZL - z, C)
    share = pl.ds(pl.multiple_of(y * fy, fy), fy)

    def nt_copy(i):
        to = i * C + mine
        return rcopy(
            nt.at[pl.ds(to * X, X), share], br.at[y, c, lax.div(z, C)],
            nt_s.at[i], nt_r.at[lax.div(z, C)], (to * X + x, m),
        )

    def partners(fn):
        def one(i, _):
            @pl.when(i * C + mine != z)
            def _():
                fn(i)

            return 0

        lax.fori_loop(0, per_class, one, 0)

    partners(lambda i: nt_copy(i).start())

    @pl.when(mine == lax.rem(z, C))
    def _():
        br[y, c, lax.div(z, C)] = nt[pl.ds(z * X, X), share]

    seg = jnp.broadcast_to(seg_ref[...].astype(F32), (ROWS, ROWS))
    attended, grads = head_pass(
        projected, qg_ref[...], kg_ref[...], seg == seg.T, cot_ref[...]
    )
    ga[z] = grads

    def z_half(level, i):
        return ga.at[level, pl.ds(i * (ROWS // 2), ROWS // 2)]

    def z_copy(level, up, i, far=False):
        step = X * EXPRESS if far else X
        dev = (d + step, m) if up else (d - step, m)
        at = level * 2 + i
        ref = z_half(level, i)
        out = at + (2 * ZL if up else 0) + (4 * ZL if far else 0)
        return rcopy(ref, ref, zg_s.at[out], zg_r.at[at], dev)

    def z_wait(level, i):
        ref = z_half(level, i)
        at = level * 2 + i
        rcopy(ref, ref, zg_s.at[at], zg_r.at[at], (lax.rem(d + X, n_dp), m)).wait_recv()

    def levels(k, fn):
        @pl.when(z >= k)
        def _():
            fn(z - k, True)

        @pl.when(z + k < ZL)
        def _():
            fn(z + k, False)

    def z_on(level, below, k, fn):
        for up in (True, False):
            if k == 0 or (below == up and k % EXPRESS != EXPRESS - 1):

                @pl.when((z < ZL - 1) if up else (z > 0))
                def _():
                    fn(level, up, False)

            if k == 0 and EXPRESS < ZL:

                @pl.when((z + EXPRESS < ZL) if up else (z >= EXPRESS))
                def _():
                    fn(level, up, True)

    def z_step(k, i):
        def one(level, below):
            z_wait(level, i)
            z_on(level, below, k, lambda level, up, far: z_copy(level, up, i, far).start())

        return one

    for i in (0, 1):
        z_on(z, None, 0, lambda level, up, far: z_copy(level, up, i, far).start())
    attn_ref[...] = attended

    order = ring_h.others() + [h]

    def term(idx):
        hh = order[idx]
        rows = Y * C * feats
        block = dot(w_ref[pl.ds(pl.multiple_of(hh * rows, rows), rows), :], grads, 1, 1)
        block = block.astype(BF16)
        for q in range(Y):
            for core in range(C):
                at = (q * C + core) * feats
                ts[hh, core, q] = block[at : at + feats]
        if C == 2:
            core_copy(idx).start()

    def core_copy(idx):
        return rcopy(ts.at[order[idx], other], cr.at[idx], ca_s.at[idx], ca_r.at[idx], twin)

    def scatter_y(idx):
        hh = order[idx]
        return Scatter(
            ring_y,
            lambda q: ts.at[hh, c, q],
            lambda q, i: ts.at[hh, c, q, pl.ds(i * (feats // 2), feats // 2)],
            [ya.at[idx], yb.at[idx], yl.at[idx], yr.at[idx]],
            yr_s, yr_r, idx,
        )

    s_y = [scatter_y(i) for i in range(len(order))]
    s_h = Scatter(
        ring_h,
        lambda q: qb.at[q],
        lambda q, i: qb.at[q, pl.ds(i * (feats // 2), feats // 2)],
        [za, zb, zl_, zr_],
        hr_s, hr_r, 0,
    )

    def rs_a(idx):
        if C == 2:
            core_copy(idx).wait_recv()
            add_to(ts.at[order[idx], c], cr.at[idx])
        s_y[idx].first()

    def rs_b(idx):
        s_y[idx].second()

    def rs_c(idx):
        qb[order[idx]] = s_y[idx].total().astype(BF16)

    for i in range(len(order)):
        term(i)

    g_n = Gather(
        ring_y,
        lambda q: br.at[q, c],
        lambda q, i: br.at[q, c, pl.ds(i * (per_class // 2), per_class // 2)],
        ny_s, ny_r, 0,
    )

    def n_copy(q, core):
        return rcopy(br.at[q, core], br.at[q, core], nc_s.at[q], nc_r.at[q], twin)

    def n_wait(i):
        ref = br.at[y, c, i]
        rcopy(ref, ref, nt_s.at[i], nt_r.at[i], (lax.rem(d + X, n_dp), m)).wait_recv()

    def n_to_twin(qs):
        if C == 2:
            for q in qs:
                n_copy(q, c).start()

    def n_first():
        partners(n_wait)
        g_n.send()
        n_to_twin([y])

    def n_second():
        g_n.relay()
        g_n.rest()
        n_to_twin(near_y)

    def n_third():
        g_n.last()
        n_to_twin(far_y)

    def n_last():
        if C == 2:
            for q in range(Y):
                n_copy(q, other).wait_recv()

    every = range(len(order))
    jobs = [
        [functools.partial(rs_a, i) for i in every] + [n_first],
        [functools.partial(rs_b, i) for i in every] + [n_second],
        [functools.partial(rs_c, i) for i in every] + [s_h.first, n_third],
        [n_last],
        [],
        [],
        [s_h.second],
    ]

    def weight_term(level, _=None):
        kind, i = lax.rem(z + level, C), lax.div(level, C)
        left = [br[:, kind, i, q].reshape(feats, ROWS) for q in range(X)]
        wa[...] += dot(jnp.concatenate(left, axis=0), ga[level], 1, 0)

    away = sorted(range(1, ZL), key=lambda k: (k // EXPRESS + k % EXPRESS, k))

    def weight_terms(first, last):
        def one(at, _):
            k = at + 1
            for i, value in enumerate(away):
                k = jnp.where(at == i, value, k)
            levels(k, weight_term)
            return 0

        lax.fori_loop(first, last, one, 0)

    wa[...] = jnp.zeros_like(wa)
    for at in range(max(len(away), len(jobs))):
        if at < len(away):
            levels(away[at], z_step(away[at], 0))
            levels(away[at], z_step(away[at], 1))
        for job in jobs[at] if at < len(jobs) else []:
            job()
        if at == 4:
            weight_term(z)
            weight_terms(0, min(at, len(away)))
    weight_terms(min(4, len(away)), len(away))
    wb[...] = wa[...].astype(BF16).reshape(wb.shape)
    s_x = Scatter(
        ring_x,
        lambda q: wb.at[q],
        lambda q, i: wb.at[q, pl.ds(i * (feats // 2), feats // 2)],
        [xa, xb, xl, xr],
        xs_s, xs_r, 0,
    )
    s_x.first()
    s_x.second()
    wg_ref[...] = s_x.total()
    ng_ref[...] = s_h.total()

    def a2a_drain(k, _):
        to = lax.rem(d + k, n_dp)
        rcopy(out_buf.at[to], arr.at[d], a2a_s.at[to], a2a_r.at[d], (to, m)).wait_send()
        return 0

    lax.fori_loop(1, n_dp, a2a_drain, 0)
    g_h.drain()
    for g in g_y:
        g.drain()
    if C == 2:
        for i, hh in enumerate(come):
            for q in range(Y):
                twin_copy(i, hh, q, c).wait_send()

    partners(lambda i: nt_copy(i).wait_send())
    g_n.drain()
    if C == 2:
        for q in range(Y):
            n_copy(q, c).wait_send()
        for i in every:
            core_copy(i).wait_send()
    for i in every:
        s_y[i].drain()
    s_h.drain()

    def z_sent(level, up, far):
        for i in (0, 1):
            z_copy(level, up, i, far).wait_send()

    z_on(z, None, 0, z_sent)
    for k in away:
        levels(k, lambda level, below: z_on(level, below, k, z_sent))
    s_x.drain()


def deliver(a_ref, b_ref, c_ref, a_out, b_out, c_out):
    a_out[...] = a_ref[...]
    b_out[...] = b_ref[...]
    c_out[...] = c_ref[...]


def on_device(
    patches, route_owner, route_slot, segment_ids, ln_gain, qkv_weight, q_gain, k_gain, d_attn
):
    n_dp, n_mp = ZL * X, ZH * Y * C
    feats = patches.shape[1]
    width = qkv_weight.shape[0]
    ext = -(-(feats + 1) // 128) * 128
    vmem = pl.BlockSpec(memory_space=pltpu.VMEM)
    dma = lambda n: pltpu.SemaphoreType.DMA((max(n, 1),))
    half = feats // 2
    pairs = []
    for n in (n_dp, 6, 6 * ZH, ZH * Y, ZL // C, 6, Y):
        pairs += [dma(n), dma(n)]
    pairs += [dma(8 * ZL), dma(2 * ZL), dma(6), dma(6)]
    for n in (ZH, 6 * ZH, 6):
        pairs += [dma(n), dma(n)]
    operands = (
        patches.T,
        route_owner.reshape(1, ROWS),
        route_slot.reshape(1, ROWS),
        segment_ids,
        ln_gain.reshape(width // 128, 128),
        qkv_weight,
        q_gain.reshape(1, HEAD),
        k_gain.reshape(1, HEAD),
        d_attn,
    )
    out_shape = (
        jax.ShapeDtypeStruct((ROWS, HEAD), BF16),
        jax.ShapeDtypeStruct((feats, ROWS), F32),
        jax.ShapeDtypeStruct((width // n_dp, 3 * HEAD), F32),
    )
    anywhere = pl.BlockSpec(memory_space=pl.ANY)
    results = pl.pallas_call(
        kernel,
        out_shape=out_shape,
        in_specs=[anywhere] * 9,
        out_specs=(vmem, vmem, vmem),
        scratch_shapes=[
            *[pltpu.VMEM(a.shape, a.dtype) for a in operands],
            pltpu.VMEM((width, 128), F32),
            pltpu.VMEM((ext, ROWS), BF16),
            pltpu.VMEM((n_dp, SLOT, ext), BF16),
            pltpu.VMEM((n_dp, SLOT, ext), BF16),
            pltpu.VMEM((n_mp, feats, ROWS), BF16),
            pltpu.VMEM((n_mp, feats, ROWS), BF16),
            pltpu.VMEM((Y, C, ZL // C, X, feats // Y, ROWS), BF16),
            pltpu.VMEM((ZL, ROWS, 3 * HEAD), BF16),
            pltpu.VMEM((ZH, C, Y, feats, ROWS), BF16),
            pltpu.VMEM((ZH, Y, feats, ROWS), BF16),
            pltpu.VMEM((ZH, half, ROWS), BF16),
            pltpu.VMEM((ZH, half, ROWS), BF16),
            pltpu.VMEM((ZH, feats, ROWS), BF16),
            pltpu.VMEM((ZH, feats, ROWS), BF16),
            pltpu.VMEM((ZH, feats, ROWS), BF16),
            pltpu.VMEM((half, ROWS), BF16),
            pltpu.VMEM((half, ROWS), BF16),
            pltpu.VMEM((feats, ROWS), BF16),
            pltpu.VMEM((feats, ROWS), BF16),
            pltpu.VMEM((X * feats, 3 * HEAD), F32),
            pltpu.VMEM((X, feats, 3 * HEAD), BF16),
            pltpu.VMEM((half, 3 * HEAD), BF16),
            pltpu.VMEM((half, 3 * HEAD), BF16),
            pltpu.VMEM((feats, 3 * HEAD), BF16),
            pltpu.VMEM((feats, 3 * HEAD), BF16),
            dma(len(operands)),
            *pairs,
        ],
        compiler_params=pltpu.CompilerParams(
            collective_id=0, has_side_effects=True, vmem_limit_bytes=62 * 1024 * 1024
        ),
    )(*operands)
    return pl.pallas_call(
        deliver,
        out_shape=out_shape,
        in_specs=[vmem] * 3,
        out_specs=(vmem,) * 3,
        compiler_params=pltpu.CompilerParams(vmem_limit_bytes=62 * 1024 * 1024),
    )(*results)


def solution(mesh):
    in_specs = (
        P("dp", "mp"),
        P("dp"),
        P("dp"),
        P("dp", None),
        P(),
        P(None, "mp"),
        P("mp"),
        P("mp"),
        P("dp", "mp"),
    )
    out_specs = (P("dp", "mp"), P("mp", "dp"), P("dp", "mp"))
    return jax.shard_map(
        on_device, mesh=mesh, in_specs=in_specs, out_specs=out_specs, check_vma=False
    )
```

```python
import functools
import math

import jax
import jax.numpy as jnp
from jax import lax
from jax.experimental import pallas as pl
from jax.experimental.pallas import tpu as pltpu
from jax.sharding import PartitionSpec as P

MESH = pl.DeviceIdType.MESH
F32 = jnp.float32
BF16 = jnp.bfloat16
HEAD = 128
ROWS = 128
ZL, X = 8, 4
ZH, Y, C = 4, 4, 2
EXPRESS = 4
SLOT = 16
HIGHEST = lax.Precision.HIGHEST


def dot(a, b, ca, cb, precision=None):
    return lax.dot_general(
        a, b, (((ca,), (cb,)), ((), ())), precision=precision, preferred_element_type=F32
    )


def rcopy(src, dst, ssem, rsem, dev):
    return pltpu.make_async_remote_copy(
        src_ref=src, dst_ref=dst, send_sem=ssem, recv_sem=rsem, device_id=dev, device_id_type=MESH
    )


class Ring:
    def __init__(self, n, p, dev):
        self.n, self.p = n, p
        self.right = lax.rem(p + 1, n)
        self.left = lax.rem(p + n - 1, n)
        self.opp = lax.rem(p + 2, n)
        self.dev_right, self.dev_left = dev(self.right), dev(self.left)

    def others(self):
        return {1: [], 2: [self.left], 4: [self.opp, self.left, self.right]}[self.n]

    def neighbours(self):
        return {1: [], 2: [self.dev_right], 4: [self.dev_left, self.dev_right]}[self.n]


class Gather:
    SENDS = 6

    def __init__(self, ring, block, half, ss, rs, base):
        self.ring, self.block, self.half = ring, block, half
        self.ss, self.rs, self.base = ss, rs, base * self.SENDS

    def _copy(self, ref, i, dev):
        return rcopy(ref, ref, self.ss.at[self.base + i], self.rs.at[self.base + i], dev)

    def _sent(self):
        g = self.ring
        if g.n == 1:
            return []
        if g.n == 2:
            return [lambda: self._copy(self.block(g.p), 0, g.dev_right)]
        return [
            lambda: self._copy(self.half(g.p, 0), 0, g.dev_right),
            lambda: self._copy(self.half(g.p, 1), 1, g.dev_left),
            lambda: self._copy(self.half(g.p, 1), 2, g.dev_right),
            lambda: self._copy(self.half(g.p, 0), 3, g.dev_left),
            lambda: self._copy(self.half(g.left, 0), 4, g.dev_right),
            lambda: self._copy(self.half(g.right, 1), 5, g.dev_left),
        ]

    def send(self):
        for copy in self._sent()[:4]:
            copy().start()

    def relay(self):
        g = self.ring
        if g.n == 4:
            sent = self._sent()
            self._copy(self.half(g.left, 0), 0, g.dev_right).wait_recv()
            sent[4]().start()
            self._copy(self.half(g.right, 1), 1, g.dev_left).wait_recv()
            sent[5]().start()

    def rest(self):
        g = self.ring
        if g.n == 2:
            self._copy(self.block(g.left), 0, g.dev_right).wait_recv()
        if g.n == 4:
            self._copy(self.half(g.left, 1), 2, g.dev_right).wait_recv()
            self._copy(self.half(g.right, 0), 3, g.dev_left).wait_recv()

    def last(self):
        g = self.ring
        if g.n == 4:
            self._copy(self.half(g.opp, 0), 4, g.dev_right).wait_recv()
            self._copy(self.half(g.opp, 1), 5, g.dev_left).wait_recv()

    def drain(self):
        for copy in self._sent():
            copy().wait_send()


class Scatter:
    SENDS = 6

    def __init__(self, ring, block, half, bufs, ss, rs, base):
        self.ring, self.block, self.half, self.bufs = ring, block, half, bufs
        self.ss, self.rs, self.base = ss, rs, base * self.SENDS

    def _copy(self, ref, dst, i, dev):
        return rcopy(ref, dst, self.ss.at[self.base + i], self.rs.at[self.base + i], dev)

    def _sent(self):
        g, b = self.ring, self.bufs
        if g.n == 1:
            return []
        if g.n == 2:
            return [lambda: self._copy(self.block(g.right), b[2], 0, g.dev_right)]
        return [
            lambda: self._copy(self.half(g.opp, 0), b[0], 0, g.dev_right),
            lambda: self._copy(self.half(g.opp, 1), b[1], 1, g.dev_left),
            lambda: self._copy(self.half(g.right, 1), self._part(b[2], 1), 2, g.dev_right),
            lambda: self._copy(self.half(g.left, 0), self._part(b[3], 0), 3, g.dev_left),
            lambda: self._copy(self.half(g.right, 0), self._part(b[2], 0), 4, g.dev_right),
            lambda: self._copy(self.half(g.left, 1), self._part(b[3], 1), 5, g.dev_left),
        ]

    @staticmethod
    def _part(ref, i):
        rows = ref.shape[0] // 2
        return ref.at[pl.ds(i * rows, rows)]

    def first(self):
        for copy in self._sent()[:4]:
            copy().start()

    def second(self):
        g = self.ring
        if g.n == 4:
            sent = self._sent()
            sent[0]().wait_recv()
            add_to(self.half(g.right, 0), self.bufs[0])
            sent[4]().start()
            sent[1]().wait_recv()
            add_to(self.half(g.left, 1), self.bufs[1])
            sent[5]().start()

    def total(self):
        g, sent = self.ring, self._sent()
        out = self.block(g.p)[...].astype(F32)
        if g.n == 2:
            sent[0]().wait_recv()
        if g.n == 4:
            for i in (2, 3, 4, 5):
                sent[i]().wait_recv()
        if g.n > 1:
            out = out + self.bufs[2][...].astype(F32)
        if g.n == 4:
            out = out + self.bufs[3][...].astype(F32)
        return out

    def drain(self):
        for copy in self._sent():
            copy().wait_send()


def add_to(ref, other):
    ref[...] = (ref[...].astype(F32) + other[...].astype(F32)).astype(ref.dtype)


def mean_of(v):
    return jnp.mean(v, axis=1, keepdims=True)


def norm_head(vector, gain_row):
    center = vector - mean_of(vector)
    inverse = lax.rsqrt(mean_of(center * center) + 1e-06)
    unit_rows = center * inverse
    return unit_rows * gain_row, unit_rows, inverse


def norm_head_back(cotangent, unit_rows, inverse, gain_row):
    scaled = cotangent * gain_row
    return inverse * (scaled - mean_of(scaled) - unit_rows * mean_of(scaled * unit_rows))


def head_pass(projected, gain_query, gain_key, allowed, cotangent):
    value_rows = projected[:, 2 * HEAD :]
    query_n, query_u, query_r = norm_head(projected[:, :HEAD].astype(F32), gain_query)
    key_n, key_u, key_r = norm_head(projected[:, HEAD : 2 * HEAD].astype(F32), gain_key)
    factor = 1.0 / math.sqrt(HEAD)
    scores = dot(query_n, key_n, 1, 1, HIGHEST) * factor
    scores = jnp.where(allowed, scores, -1e30)
    shifted = jnp.exp(scores - jnp.max(scores, axis=1, keepdims=True))
    softmax_rows = shifted / jnp.sum(shifted, axis=1, keepdims=True)
    probs_low = softmax_rows.astype(BF16)
    attended = dot(probs_low, value_rows, 1, 0).astype(BF16)
    grad_value = dot(probs_low, cotangent, 0, 0)
    grad_probs = dot(cotangent, value_rows, 1, 1)
    grad_scores = softmax_rows * (
        grad_probs - jnp.sum(grad_probs * softmax_rows, axis=1, keepdims=True)
    )
    grad_qn = dot(grad_scores, key_n, 1, 0, HIGHEST) * factor
    grad_kn = dot(grad_scores, query_n, 0, 0, HIGHEST) * factor
    grad_query = norm_head_back(grad_qn, query_u, query_r, gain_query)
    grad_key = norm_head_back(grad_kn, key_u, key_r, gain_key)
    return attended, jnp.concatenate([grad_query, grad_key, grad_value], axis=1).astype(BF16)


def kernel(
    patches_hbm, owner_hbm, slot_hbm, seg_hbm, gain_hbm, w_hbm, qg_hbm, kg_hbm, cot_hbm,
    attn_ref, ng_ref, wg_ref,
    patches_ref, owner_ref, slot_ref, seg_ref, gain_ref, w_ref, qg_ref, kg_ref, cot_ref,
    gb_ref, pt_ref, out_buf, arr, gath, nt, br, ga, ts, cr, ya, yb, yl, yr, qb, za, zb, zl_, zr_,
    wa, wb, xa, xb, xl, xr,
    in_sem, a2a_s, a2a_r, hg_s, hg_r, yg_s, yg_r, cg_s, cg_r, nt_s, nt_r, ny_s, ny_r, nc_s, nc_r,
    zg_s, zg_r, xs_s, xs_r, ca_s, ca_r, yr_s, yr_r, hr_s, hr_r,
):
    n_dp, n_mp = ZL * X, ZH * Y * C
    feats = patches_hbm.shape[0]
    width = n_mp * feats
    fy = feats // Y
    per_class = ZL // C
    d, m = lax.axis_index("dp"), lax.axis_index("mp")
    z, x = lax.div(d, X), lax.rem(d, X)
    h, y, c = lax.div(m, Y * C), lax.rem(lax.div(m, C), Y), lax.rem(m, C)
    ring_h = Ring(ZH, h, lambda q: (d, (q * Y + y) * C + c))
    ring_y = Ring(Y, y, lambda q: (d, (h * Y + q) * C + c))
    ring_x = Ring(X, x, lambda q: (z * X + q, m))
    twin = (d, (h * Y + y) * C + (1 - c))
    other = 1 - c

    loads = [
        pltpu.make_async_copy(src, dst, in_sem.at[i])
        for i, (src, dst) in enumerate([
            (owner_hbm, owner_ref), (patches_hbm, patches_ref), (slot_hbm, slot_ref),
            (gain_hbm, gain_ref), (seg_hbm, seg_ref), (qg_hbm, qg_ref), (kg_hbm, kg_ref),
            (cot_hbm, cot_ref), (w_hbm, w_ref),
        ])
    ]
    for load in loads:
        load.start()

    barrier = pltpu.get_barrier_semaphore()

    def hail(k, _):
        to = lax.rem(d + k, n_dp)
        pl.semaphore_signal(barrier, inc=1, device_id=(to, m), device_id_type=MESH)
        return 0

    lax.fori_loop(1, n_dp, hail, 0)
    near = ring_h.neighbours() + ring_y.neighbours() + ([twin] if C == 2 else [])
    for dev in near:
        pl.semaphore_signal(barrier, inc=1, device_id=dev, device_id_type=MESH)

    for load in loads[:4]:
        load.wait()
    owners = jnp.broadcast_to(owner_ref[...].astype(F32), (ROWS, ROWS))
    rows_i = lax.broadcasted_iota(jnp.int32, (ROWS, ROWS), 0)
    cols_i = lax.broadcasted_iota(jnp.int32, (ROWS, ROWS), 1)
    same = jnp.where((owners == owners.T) & (rows_i < cols_i), 1.0, 0.0)
    rank = jnp.sum(same, axis=0, keepdims=True)
    target = owner_ref[...].astype(F32) * SLOT + rank
    slots_i = lax.broadcasted_iota(jnp.int32, (n_dp * SLOT, ROWS), 0).astype(F32)
    pick = jnp.where(slots_i == target, 1.0, 0.0).astype(BF16)
    pt_ref[:feats] = patches_ref[...]
    pt_ref[feats:] = jnp.broadcast_to(
        slot_ref[...].astype(F32) + 1.0, (pt_ref.shape[0] - feats, ROWS)
    ).astype(BF16)
    outgoing = dot(pick, pt_ref[...], 1, 1).astype(BF16)
    out_buf[...] = outgoing.reshape(out_buf.shape)

    pl.semaphore_wait(barrier, n_dp - 1 + len(near))

    def a2a_send(k, _):
        to = lax.rem(d + k, n_dp)
        rcopy(out_buf.at[to], arr.at[d], a2a_s.at[to], a2a_r.at[d], (to, m)).start()
        return 0

    lax.fori_loop(1, n_dp, a2a_send, 0)
    arr[d] = out_buf[d]

    def spread_gain(j, _):
        tile = jnp.broadcast_to(gain_ref[pl.ds(j, 1), :], (128, 128))
        gb_ref[pl.ds(pl.multiple_of(j * 128, 128), 128), :] = tile.T
        return 0

    lax.fori_loop(0, width // 128, spread_gain, 0)

    def a2a_wait(k, _):
        frm = lax.rem(d + n_dp - k, n_dp)
        rcopy(out_buf.at[frm], arr.at[frm], a2a_s.at[frm], a2a_r.at[frm], (frm, m)).wait_recv()
        return 0

    lax.fori_loop(1, n_dp, a2a_wait, 0)
    arrived = arr[...].reshape(n_dp * SLOT, arr.shape[2])
    lanes = lax.broadcasted_iota(jnp.int32, (n_dp * SLOT, ROWS), 1).astype(F32) + 1.0
    place = jnp.where(
        lanes == arrived[:, feats : feats + 1].astype(F32), 1.0, 0.0
    ).astype(BF16)
    gath[m] = dot(arrived[:, :feats], place, 0, 0).astype(BF16)

    g_h = Gather(
        ring_h,
        lambda q: gath.at[(q * Y + y) * C + c],
        lambda q, i: gath.at[(q * Y + y) * C + c, pl.ds(i * (feats // 2), feats // 2)],
        hg_s, hg_r, 0,
    )

    def gather_y(idx, hh):
        return Gather(
            ring_y,
            lambda q: gath.at[(hh * Y + q) * C + c],
            lambda q, i: gath.at[(hh * Y + q) * C + c, pl.ds(i * (feats // 2), feats // 2)],
            yg_s, yg_r, idx,
        )

    def twin_copy(idx, hh, q, core):
        ref = gath.at[(hh * Y + q) * C + core]
        i = idx * Y + q
        return rcopy(ref, ref, cg_s.at[i], cg_r.at[i], twin)

    def to_twin(idx, hh, qs):
        if C == 2:
            for q in qs:
                twin_copy(idx, hh, q, c).start()

    come = [h] + {1: [], 2: [ring_h.left], 4: [ring_h.left, ring_h.right, ring_h.opp]}[ZH]
    g_y = [gather_y(i, hh) for i, hh in enumerate(come)]
    near_y = {1: [], 2: [ring_y.left], 4: [ring_y.left, ring_y.right]}[Y]
    far_y = [ring_y.opp] if Y == 4 else []

    def own_y(i):
        g_y[i].send()
        to_twin(i, come[i], [y])

    def next_y(i):
        g_y[i].relay()
        g_y[i].rest()
        to_twin(i, come[i], near_y)

    def last_y(i):
        g_y[i].last()
        to_twin(i, come[i], far_y)

    g_h.send()
    own_y(0)
    next_y(0)
    g_h.relay()
    last_y(0)
    g_h.rest()
    near_h = range(1, min(len(come), 3))
    for i in near_h:
        own_y(i)
    for i in near_h:
        next_y(i)
    for i in near_h:
        last_y(i)
    g_h.last()
    if ZH == 4:
        own_y(3)
        next_y(3)
        last_y(3)
    if C == 2:
        for i, hh in enumerate(come):
            for q in range(Y):
                twin_copy(i, hh, q, other).wait_recv()

    def sums(j, carry):
        s1, s2 = carry
        v = gath[j].astype(F32).reshape(feats // 8, 8, ROWS)
        return s1 + jnp.sum(v, axis=0), s2 + jnp.sum(v * v, axis=0)

    zero = jnp.zeros((8, ROWS), F32)
    s1, s2 = lax.fori_loop(0, n_mp, sums, (zero, zero))
    row_mean = jnp.sum(s1, axis=0, keepdims=True) / width
    row_var = jnp.sum(s2, axis=0, keepdims=True) / width - row_mean * row_mean
    inverse = lax.rsqrt(row_var + 1e-06)

    for load in loads[4:]:
        load.wait()
    step = 4

    def project(j, acc):
        v = gath[pl.ds(j * step, step)].astype(F32).reshape(step * feats, ROWS)
        rows = pl.ds(pl.multiple_of(j * (step * feats), step * feats), step * feats)
        low = ((v - row_mean) * inverse * gb_ref[rows, :]).astype(BF16)
        nt[pl.ds(j * step, step)] = low.reshape(step, feats, ROWS)
        return acc + dot(low, w_ref[rows, :], 0, 0)

    projected = lax.fori_loop(
        0, n_mp // step, project, jnp.zeros((ROWS, 3 * HEAD), F32)
    ).astype(BF16)

    mine = lax.rem(c + C * ZL - z, C)
    share = pl.ds(pl.multiple_of(y * fy, fy), fy)

    def nt_copy(i):
        to = i * C + mine
        return rcopy(
            nt.at[pl.ds(to * X, X), share], br.at[y, c, lax.div(z, C)],
            nt_s.at[i], nt_r.at[lax.div(z, C)], (to * X + x, m),
        )

    def partners(fn):
        def one(i, _):
            @pl.when(i * C + mine != z)
            def _():
                fn(i)

            return 0

        lax.fori_loop(0, per_class, one, 0)

    partners(lambda i: nt_copy(i).start())

    @pl.when(mine == lax.rem(z, C))
    def _():
        br[y, c, lax.div(z, C)] = nt[pl.ds(z * X, X), share]

    seg = jnp.broadcast_to(seg_ref[...].astype(F32), (ROWS, ROWS))
    attended, grads = head_pass(
        projected, qg_ref[...], kg_ref[...], seg == seg.T, cot_ref[...]
    )
    ga[z] = grads

    def z_half(level, i):
        return ga.at[level, pl.ds(i * (ROWS // 2), ROWS // 2)]

    def z_copy(level, up, i, far=False):
        step = X * EXPRESS if far else X
        dev = (d + step, m) if up else (d - step, m)
        at = level * 2 + i
        ref = z_half(level, i)
        out = at + (2 * ZL if up else 0) + (4 * ZL if far else 0)
        return rcopy(ref, ref, zg_s.at[out], zg_r.at[at], dev)

    def z_wait(level, i):
        ref = z_half(level, i)
        at = level * 2 + i
        rcopy(ref, ref, zg_s.at[at], zg_r.at[at], (lax.rem(d + X, n_dp), m)).wait_recv()

    def levels(k, fn):
        @pl.when(z >= k)
        def _():
            fn(z - k, True)

        @pl.when(z + k < ZL)
        def _():
            fn(z + k, False)

    def z_on(level, below, k, fn):
        for up in (True, False):
            if k == 0 or (below == up and k % EXPRESS != EXPRESS - 1):

                @pl.when((z < ZL - 1) if up else (z > 0))
                def _():
                    fn(level, up, False)

            if k == 0 and EXPRESS < ZL:

                @pl.when((z + EXPRESS < ZL) if up else (z >= EXPRESS))
                def _():
                    fn(level, up, True)

    def z_step(k, i):
        def one(level, below):
            z_wait(level, i)
            z_on(level, below, k, lambda level, up, far: z_copy(level, up, i, far).start())

        return one

    for i in (0, 1):
        z_on(z, None, 0, lambda level, up, far: z_copy(level, up, i, far).start())
    attn_ref[...] = attended

    order = ring_h.others() + [h]

    def term(idx):
        hh = order[idx]
        rows = Y * C * feats
        block = dot(w_ref[pl.ds(pl.multiple_of(hh * rows, rows), rows), :], grads, 1, 1)
        block = block.astype(BF16)
        for q in range(Y):
            for core in range(C):
                at = (q * C + core) * feats
                ts[hh, core, q] = block[at : at + feats]
        if C == 2:
            core_copy(idx).start()

    def core_copy(idx):
        return rcopy(ts.at[order[idx], other], cr.at[idx], ca_s.at[idx], ca_r.at[idx], twin)

    def scatter_y(idx):
        hh = order[idx]
        return Scatter(
            ring_y,
            lambda q: ts.at[hh, c, q],
            lambda q, i: ts.at[hh, c, q, pl.ds(i * (feats // 2), feats // 2)],
            [ya.at[idx], yb.at[idx], yl.at[idx], yr.at[idx]],
            yr_s, yr_r, idx,
        )

    s_y = [scatter_y(i) for i in range(len(order))]
    s_h = Scatter(
        ring_h,
        lambda q: qb.at[q],
        lambda q, i: qb.at[q, pl.ds(i * (feats // 2), feats // 2)],
        [za, zb, zl_, zr_],
        hr_s, hr_r, 0,
    )

    def rs_a(idx):
        if C == 2:
            core_copy(idx).wait_recv()
            add_to(ts.at[order[idx], c], cr.at[idx])
        s_y[idx].first()

    def rs_b(idx):
        s_y[idx].second()

    def rs_c(idx):
        qb[order[idx]] = s_y[idx].total().astype(BF16)

    for i in range(len(order)):
        term(i)

    g_n = Gather(
        ring_y,
        lambda q: br.at[q, c],
        lambda q, i: br.at[q, c, pl.ds(i * (per_class // 2), per_class // 2)],
        ny_s, ny_r, 0,
    )

    def n_copy(q, core):
        return rcopy(br.at[q, core], br.at[q, core], nc_s.at[q], nc_r.at[q], twin)

    def n_wait(i):
        ref = br.at[y, c, i]
        rcopy(ref, ref, nt_s.at[i], nt_r.at[i], (lax.rem(d + X, n_dp), m)).wait_recv()

    def n_to_twin(qs):
        if C == 2:
            for q in qs:
                n_copy(q, c).start()

    def n_first():
        partners(n_wait)
        g_n.send()
        n_to_twin([y])

    def n_second():
        g_n.relay()
        g_n.rest()
        n_to_twin(near_y)

    def n_third():
        g_n.last()
        n_to_twin(far_y)

    def n_last():
        if C == 2:
            for q in range(Y):
                n_copy(q, other).wait_recv()

    every = range(len(order))
    jobs = [
        [functools.partial(rs_a, i) for i in every] + [n_first],
        [functools.partial(rs_b, i) for i in every] + [n_second],
        [functools.partial(rs_c, i) for i in every] + [s_h.first, n_third],
        [n_last],
        [],
        [],
        [s_h.second],
    ]

    def weight_term(level, _=None):
        kind, i = lax.rem(z + level, C), lax.div(level, C)
        left = [br[:, kind, i, q].reshape(feats, ROWS) for q in range(X)]
        wa[...] += dot(jnp.concatenate(left, axis=0), ga[level], 1, 0)

    away = sorted(range(1, ZL), key=lambda k: (k // EXPRESS + k % EXPRESS, k))

    def weight_terms(first, last):
        def one(at, _):
            k = at + 1
            for i, value in enumerate(away):
                k = jnp.where(at == i, value, k)
            levels(k, weight_term)
            return 0

        lax.fori_loop(first, last, one, 0)

    wa[...] = jnp.zeros_like(wa)
    for at in range(max(len(away), len(jobs))):
        if at < len(away):
            levels(away[at], z_step(away[at], 0))
            levels(away[at], z_step(away[at], 1))
        for job in jobs[at] if at < len(jobs) else []:
            job()
        if at == 4:
            weight_term(z)
            weight_terms(0, min(at, len(away)))
    weight_terms(min(4, len(away)), len(away))
    wb[...] = wa[...].astype(BF16).reshape(wb.shape)
    s_x = Scatter(
        ring_x,
        lambda q: wb.at[q],
        lambda q, i: wb.at[q, pl.ds(i * (feats // 2), feats // 2)],
        [xa, xb, xl, xr],
        xs_s, xs_r, 0,
    )
    s_x.first()
    def a2a_drain(k, _):
        to = lax.rem(d + k, n_dp)
        rcopy(out_buf.at[to], arr.at[d], a2a_s.at[to], a2a_r.at[d], (to, m)).wait_send()
        return 0

    lax.fori_loop(1, n_dp, a2a_drain, 0)
    g_h.drain()
    for g in g_y:
        g.drain()
    if C == 2:
        for i, hh in enumerate(come):
            for q in range(Y):
                twin_copy(i, hh, q, c).wait_send()

    partners(lambda i: nt_copy(i).wait_send())
    g_n.drain()
    if C == 2:
        for q in range(Y):
            n_copy(q, c).wait_send()
        for i in every:
            core_copy(i).wait_send()
    for i in every:
        s_y[i].drain()
    s_x.second()
    wg_ref[...] = s_x.total()
    ng_ref[...] = s_h.total()

    s_h.drain()

    def z_sent(level, up, far):
        for i in (0, 1):
            z_copy(level, up, i, far).wait_send()

    z_on(z, None, 0, z_sent)
    for k in away:
        levels(k, lambda level, below: z_on(level, below, k, z_sent))
    s_x.drain()


def deliver(a_ref, b_ref, c_ref, a_out, b_out, c_out):
    a_out[...] = a_ref[...]
    b_out[...] = b_ref[...]
    c_out[...] = c_ref[...]


def on_device(
    patches, route_owner, route_slot, segment_ids, ln_gain, qkv_weight, q_gain, k_gain, d_attn
):
    n_dp, n_mp = ZL * X, ZH * Y * C
    feats = patches.shape[1]
    width = qkv_weight.shape[0]
    ext = -(-(feats + 1) // 128) * 128
    vmem = pl.BlockSpec(memory_space=pltpu.VMEM)
    dma = lambda n: pltpu.SemaphoreType.DMA((max(n, 1),))
    half = feats // 2
    pairs = []
    for n in (n_dp, 6, 6 * ZH, ZH * Y, ZL // C, 6, Y):
        pairs += [dma(n), dma(n)]
    pairs += [dma(8 * ZL), dma(2 * ZL), dma(6), dma(6)]
    for n in (ZH, 6 * ZH, 6):
        pairs += [dma(n), dma(n)]
    operands = (
        patches.T,
        route_owner.reshape(1, ROWS),
        route_slot.reshape(1, ROWS),
        segment_ids,
        ln_gain.reshape(width // 128, 128),
        qkv_weight,
        q_gain.reshape(1, HEAD),
        k_gain.reshape(1, HEAD),
        d_attn,
    )
    out_shape = (
        jax.ShapeDtypeStruct((ROWS, HEAD), BF16),
        jax.ShapeDtypeStruct((feats, ROWS), F32),
        jax.ShapeDtypeStruct((width // n_dp, 3 * HEAD), F32),
    )
    anywhere = pl.BlockSpec(memory_space=pl.ANY)
    results = pl.pallas_call(
        kernel,
        out_shape=out_shape,
        in_specs=[anywhere] * 9,
        out_specs=(vmem, vmem, vmem),
        scratch_shapes=[
            *[pltpu.VMEM(a.shape, a.dtype) for a in operands],
            pltpu.VMEM((width, 128), F32),
            pltpu.VMEM((ext, ROWS), BF16),
            pltpu.VMEM((n_dp, SLOT, ext), BF16),
            pltpu.VMEM((n_dp, SLOT, ext), BF16),
            pltpu.VMEM((n_mp, feats, ROWS), BF16),
            pltpu.VMEM((n_mp, feats, ROWS), BF16),
            pltpu.VMEM((Y, C, ZL // C, X, feats // Y, ROWS), BF16),
            pltpu.VMEM((ZL, ROWS, 3 * HEAD), BF16),
            pltpu.VMEM((ZH, C, Y, feats, ROWS), BF16),
            pltpu.VMEM((ZH, Y, feats, ROWS), BF16),
            pltpu.VMEM((ZH, half, ROWS), BF16),
            pltpu.VMEM((ZH, half, ROWS), BF16),
            pltpu.VMEM((ZH, feats, ROWS), BF16),
            pltpu.VMEM((ZH, feats, ROWS), BF16),
            pltpu.VMEM((ZH, feats, ROWS), BF16),
            pltpu.VMEM((half, ROWS), BF16),
            pltpu.VMEM((half, ROWS), BF16),
            pltpu.VMEM((feats, ROWS), BF16),
            pltpu.VMEM((feats, ROWS), BF16),
            pltpu.VMEM((X * feats, 3 * HEAD), F32),
            pltpu.VMEM((X, feats, 3 * HEAD), BF16),
            pltpu.VMEM((half, 3 * HEAD), BF16),
            pltpu.VMEM((half, 3 * HEAD), BF16),
            pltpu.VMEM((feats, 3 * HEAD), BF16),
            pltpu.VMEM((feats, 3 * HEAD), BF16),
            dma(len(operands)),
            *pairs,
        ],
        compiler_params=pltpu.CompilerParams(
            collective_id=0, has_side_effects=True, vmem_limit_bytes=62 * 1024 * 1024
        ),
    )(*operands)
    return pl.pallas_call(
        deliver,
        out_shape=out_shape,
        in_specs=[vmem] * 3,
        out_specs=(vmem,) * 3,
        compiler_params=pltpu.CompilerParams(vmem_limit_bytes=62 * 1024 * 1024),
    )(*results)


def solution(mesh):
    in_specs = (
        P("dp", "mp"),
        P("dp"),
        P("dp"),
        P("dp", None),
        P(),
        P(None, "mp"),
        P("mp"),
        P("mp"),
        P("dp", "mp"),
    )
    out_specs = (P("dp", "mp"), P("mp", "dp"), P("dp", "mp"))
    return jax.shard_map(
        on_device, mesh=mesh, in_specs=in_specs, out_specs=out_specs, check_vma=False
    )
```
